32 devices in a mesh: groups: 2 (over x), dp: 8 (over z, y), tensor: 2 (over core).
Axes of the slice: x: 2, y: 2, z: 4, core: 2. Of those that a mesh axis runs over, the one named last changes fastest.
Arguments:
- tokens: bfloat16 [8192, 5120], P(('groups', 'dp'), 'tensor'), parts along dimension 0, may hold values from -6 to 6
- frozen_value_weight: bfloat16 [5120, 768], P('tensor'), may hold values from -0.078125 to 0.078125
- adapter_down_weight: bfloat16 [128, 16, 5120], P('dp', None, 'tensor'), may hold values from -0.078125 to 0.078125
- adapter_up_weight: bfloat16 [128, 16, 768], P('dp'), may hold values from -0.25 to 2
- segment_adapter_index: int32 [512], P(('groups', 'dp')), parts along dimension 0, may hold values from 0 to 127, as said below
- segment_live_length: int32 [512], P(('groups', 'dp')), parts along dimension 0, may hold values from 1 to 16
- cotangent: bfloat16 [8192, 768], P(('groups', 'dp')), parts along dimension 0, may hold values from -3 to 7.5
Outputs:
- output: bfloat16 [8192, 768], P(('groups', 'dp'), 'tensor'), parts along dimension 0
- input_gradient: bfloat16 [8192, 5120], P(('groups', 'dp'), 'tensor'), parts along dimension 0
- grad_down: bfloat16 [256, 16, 5120], P(('groups', 'dp'), None, 'tensor'), parts along dimension 0
- grad_up: bfloat16 [256, 16, 768], P(('groups', 'dp'), None, 'tensor'), parts along dimension 0
The draws below stay inside these ranges and needn't reach their ends.
There are 2 independent parts, one for each index of `groups`. The reference program is written for one: setup_inputs(seed, part) draws one part's arguments, and reference() takes and returns one part's arrays. A program takes and returns all parts, laid end to end along the dimension named above; an argument that names none is the same for every part. Nothing has to cross between parts.
Inputs may be any that keep to these rules, and one draw needn't show every extreme that they name: `segment_adapter_index`: adapter b is owned by index b // 16 of dp. Among the 32 segments of one device (aligned blocks), at most 4 name adapters of any one owner, and on every device some owner is named by exactly 4 of them.
All inputs are finite; a program needn't handle non-finite values.
Results may differ from the reference program's by a relative error of at most 0.0052.
Values may be sent and summed in bfloat16 or wider, within the bound.
A program may use at most 128 MiB of HBM per device.

```python
import jax
import jax.numpy as jnp

MODEL_WIDTH = 5120
VALUE_OUTPUTS = 768
ADAPTER_RANK = 16
ADAPT_DEV = 16
SEG_LEN = 16
SEG_DEV = 32
CAP = 4
SEGMENTS = 256
TOKEN_SLOTS = 4096
ADAPTER_TOTAL = 128


def draw_segment_adapter_index(key, part):
    key = jax.random.fold_in(key, 11)
    devices = SEGMENTS // SEG_DEV
    slot_total = devices * CAP
    first_key, second_key = jax.random.split(key, 2)
    device_keys = jax.random.split(first_key, devices)
    orders = jax.vmap(lambda one_key: jax.random.permutation(one_key, slot_total))(device_keys)
    owners_of = orders[:, :SEG_DEV] // CAP
    local_index = jax.random.randint(second_key, (devices, SEG_DEV), 0, ADAPT_DEV)
    return (owners_of * ADAPT_DEV + local_index).reshape(SEGMENTS).astype(jnp.int32)


def draw_segment_live_length(key, part):
    key = jax.random.fold_in(key, 13)
    raw_length = jax.random.randint(key, (SEGMENTS,), 1, 2 * SEG_LEN)
    return jnp.minimum(raw_length, SEG_LEN).astype(jnp.int32)


def draw_cotangent(key, part):
    key = jax.random.fold_in(key, 17)
    noise_key, peak_key = jax.random.split(key, 2)
    noise = jnp.clip(0.5 * jax.random.normal(noise_key, (TOKEN_SLOTS, VALUE_OUTPUTS), jnp.float32), -3.0, 3.0)
    slot_of_row = jnp.arange(TOKEN_SLOTS, dtype=jnp.int32) % SEG_LEN
    column_ids = jnp.arange(VALUE_OUTPUTS, dtype=jnp.int32)
    spacing = VALUE_OUTPUTS // SEG_LEN
    marked = (column_ids[None, :] == slot_of_row[:, None] * spacing).astype(jnp.float32)
    height = jax.random.uniform(peak_key, (TOKEN_SLOTS, 1), jnp.float32, 3.5, 4.5)
    return (noise + marked * height).astype(jnp.bfloat16)


def draw_adapter_up_weight(key, part):
    key = jax.random.fold_in(key, 19)
    noise_key, peak_key = jax.random.split(key, 2)
    shape = (ADAPTER_TOTAL, ADAPTER_RANK, VALUE_OUTPUTS)
    noise = jax.random.normal(noise_key, shape, jnp.float32) * (1.0 / VALUE_OUTPUTS) ** 0.5
    noise = jnp.clip(noise, -0.25, 0.25)
    rank_ids = jnp.arange(ADAPTER_RANK, dtype=jnp.int32)
    column_ids = jnp.arange(VALUE_OUTPUTS, dtype=jnp.int32)
    spacing = VALUE_OUTPUTS // ADAPTER_RANK
    marked = (column_ids[None, :] == rank_ids[:, None] * spacing).astype(jnp.float32)[None, :, :]
    height = jax.random.uniform(peak_key, (ADAPTER_TOTAL, ADAPTER_RANK, 1), jnp.float32, 1.25, 1.75)
    return (noise + marked * height).astype(jnp.bfloat16)


def block_levels(key, extent, cuts, smallest, top_value):
    level, own = 1.0, jax.random.fold_in(key, 6)
    for position, shards_of in cuts:
        steps = jnp.exp(jax.random.uniform(jax.random.fold_in(own, position), (shards_of,), jnp.float32, smallest / len(cuts), top_value / len(cuts)))
        level = level * jnp.repeat(steps, extent[position] // shards_of).reshape([-1 if axis == position else 1 for axis in range(len(extent))])
    return level


def scatter_about(own_key, extent, width, reach, shards=(), held_as=jnp.bfloat16):
    level = block_levels(own_key, extent, shards, -0.22, 0.18) if shards else 1.0
    drawn = jax.random.normal(own_key, extent, jnp.float32) * width * level
    return jnp.minimum(jnp.maximum(drawn, -reach), reach).astype(held_as)


def setup_inputs(seed: int = 0, part: int = 0) -> dict:
    seeds = jax.random.split(jax.random.key(seed), 8)
    own_keys = jax.random.split(jax.random.fold_in(seeds[7], part), 8)
    return {
        "tokens": scatter_about(own_keys[0], (TOKEN_SLOTS, MODEL_WIDTH), 1.0, 6.0, ((0, 8), (1, 2))),
        "frozen_value_weight": scatter_about(seeds[1], (MODEL_WIDTH, VALUE_OUTPUTS), MODEL_WIDTH ** -0.5, 0.078125, ((0, 2),)),
        "adapter_down_weight": scatter_about(seeds[2], (ADAPTER_TOTAL, ADAPTER_RANK, MODEL_WIDTH), MODEL_WIDTH ** -0.5, 0.078125, ((0, 8), (2, 2))),
        "adapter_up_weight": draw_adapter_up_weight(jax.random.fold_in(seeds[7], 71), part),
        "segment_adapter_index": draw_segment_adapter_index(jax.random.fold_in(jax.random.fold_in(seeds[7], part), 71), part),
        "segment_live_length": draw_segment_live_length(jax.random.fold_in(jax.random.fold_in(seeds[7], part), 71), part),
        "cotangent": draw_cotangent(jax.random.fold_in(jax.random.fold_in(seeds[7], part), 71), part),
    }


adapter_scale = 2.0


def reference(tokens, frozen_value_weight, adapter_down_weight, adapter_up_weight, segment_adapter_index, segment_live_length, cotangent):
    token_seg = tokens.reshape(SEGMENTS, SEG_LEN, MODEL_WIDTH).astype(jnp.float32)
    segment_output_gradient = cotangent.reshape(SEGMENTS, SEG_LEN, VALUE_OUTPUTS).astype(jnp.float32)
    slot_pos = jnp.arange(SEG_LEN, dtype=jnp.int32)
    active_token_mask = (slot_pos[None, :] < segment_live_length[:, None]).astype(jnp.float32)[:, :, None]
    segment_down_weight = adapter_down_weight[segment_adapter_index].astype(jnp.float32)
    segment_up_weight = adapter_up_weight[segment_adapter_index].astype(jnp.float32)
    reduced_activations = (jnp.einsum("std,srd->str", token_seg, segment_down_weight) * active_token_mask).astype(jnp.bfloat16)
    frozen_output_sum = jnp.dot(tokens, frozen_value_weight, preferred_element_type=jnp.float32).reshape(SEGMENTS, SEG_LEN, VALUE_OUTPUTS)
    expand_rank = jnp.einsum("str,sro->sto", reduced_activations.astype(jnp.float32), segment_up_weight)
    output = (frozen_output_sum + adapter_scale * expand_rank).astype(jnp.bfloat16).reshape(TOKEN_SLOTS, VALUE_OUTPUTS)
    reduced_gradient = (adapter_scale * jnp.einsum("wad,wzd->waz", segment_output_gradient, segment_up_weight) * active_token_mask).astype(jnp.bfloat16)
    frozen_backward = jnp.dot(cotangent, frozen_value_weight.T, preferred_element_type=jnp.float32)
    adapter_backward = jnp.einsum("omg,ogv->omv", reduced_gradient.astype(jnp.float32), segment_down_weight).reshape(TOKEN_SLOTS, MODEL_WIDTH)
    input_gradient = (frozen_backward + adapter_backward).astype(jnp.bfloat16)
    down_terms = jnp.einsum("str,std->srd", reduced_gradient.astype(jnp.float32), token_seg)
    up_projection_terms = adapter_scale * jnp.einsum("ubd,ubp->udp", reduced_activations.astype(jnp.float32), segment_output_gradient)
    grad_down = jax.ops.segment_sum(down_terms, segment_adapter_index, num_segments=ADAPTER_TOTAL).astype(jnp.bfloat16)
    grad_up = jax.ops.segment_sum(up_projection_terms, segment_adapter_index, num_segments=ADAPTER_TOTAL).astype(jnp.bfloat16)
    return output, input_gradient, grad_down, grad_up
```

```python
import jax
import jax.numpy as jnp
from jax import lax
from jax.sharding import PartitionSpec as P

adapter_scale = 2.0
BF = jnp.bfloat16
F32 = jnp.float32


def mm(a, b, ca=1, cb=0, **kw):
    return lax.dot_general(
        a, b, (((ca,), (cb,)), ((), ())), preferred_element_type=F32, **kw
    )


def local(tokens, weight, down, up, index, length, cot):
    dp = lax.axis_size("dp")
    seg_dev = index.shape[0]
    rows, half_d = tokens.shape
    seg_len = rows // seg_dev
    full_out = weight.shape[1]
    half_out = full_out // lax.axis_size("tensor")
    n_own, rank = down.shape[0], down.shape[1]
    per_owner = max(1, -(-seg_dev // dp))
    n_slots = dp * per_owner
    n_tok, n_rank, n_ad = n_slots * seg_len, n_slots * rank, n_own * rank
    column = lax.axis_index("tensor") * half_out

    owners = index // n_own
    local_index = index - owners * n_own
    pos = jnp.arange(seg_dev, dtype=jnp.int32)
    earlier = (owners[:, None] == owners[None, :]) & (pos[None, :] < pos[:, None])
    placed = owners * per_owner + jnp.sum(earlier.astype(jnp.int32), axis=1)
    picker = placed[None, :] == jnp.arange(n_slots, dtype=jnp.int32)[:, None]
    request = jnp.sum(jnp.where(picker, local_index[None, :] + 1, 0), axis=1)
    requested = (
        lax.all_to_all(
            request.reshape(dp, per_owner), "dp", split_axis=0, concat_axis=0, tiled=True
        ).reshape(n_slots)
        - 1
    )

    row_i = jnp.arange(rows, dtype=jnp.int32)
    placed_row = jnp.repeat(placed, seg_len)
    dest = placed_row * seg_len + row_i % seg_len
    live = (row_i % seg_len < jnp.repeat(length, seg_len)).astype(F32)[:, None]
    tok_i = jnp.arange(n_tok, dtype=jnp.int32)
    rank_i = jnp.arange(n_rank, dtype=jnp.int32)
    ad_i = jnp.arange(n_ad, dtype=jnp.int32)
    r_i = jnp.arange(rank, dtype=jnp.int32)
    place = (tok_i[:, None] == dest[None, :]).astype(BF)
    source = jnp.repeat(requested, rank) * rank + rank_i % rank
    choose = (source[:, None] == ad_i[None, :]).astype(BF)
    own_block = placed_row[:, None] == (rank_i // rank)[None, :]
    ad_block = jnp.repeat(requested, seg_len)[:, None] == (ad_i // rank)[None, :]
    spread = (rank_i[None, :] % rank == r_i[:, None]).astype(BF)
    spread_ad = (ad_i[None, :] % rank == r_i[:, None]).astype(BF)

    def exchange(x):
        y = lax.all_to_all(
            x.reshape(dp, x.shape[0] // dp, x.shape[1]),
            "dp", split_axis=0, concat_axis=0, tiled=True,
        )
        return y.reshape(x.shape)

    cot_half = lax.dynamic_slice_in_dim(cot, column, half_out, 1)
    up2 = lax.dynamic_slice_in_dim(up.reshape(n_ad, full_out), column, half_out, 1)
    tok_got = exchange(mm(place, tokens).astype(BF))
    cot_got = exchange(mm(place, cot_half).astype(BF))
    up_got = exchange(mm(choose, up2).astype(BF))
    down_got = exchange(mm(choose, down.reshape(n_ad, half_d)).astype(BF))

    base = lax.psum_scatter(mm(tokens, weight), "tensor", scatter_dimension=1, tiled=True)

    def compact(full):
        masked = jnp.where(own_block, full, 0.0)
        return mm(masked, spread.astype(F32), 1, 1, precision=lax.Precision.HIGHEST)

    parts = jnp.concatenate(
        [compact(mm(tokens, down_got, 1, 1)), compact(mm(cot_half, up_got, 1, 1))], axis=1
    )
    sums = lax.psum(parts, "tensor") * live
    shrunk = sums[:, :rank].astype(BF)
    d_shrunk = (adapter_scale * sums[:, rank:]).astype(BF)
    both = jnp.concatenate([shrunk, d_shrunk], axis=1)
    both_got = exchange(mm(place, both).astype(BF))

    shrunk_wide = jnp.where(own_block, mm(shrunk, spread), 0.0).astype(BF)
    d_wide = jnp.where(own_block, mm(d_shrunk, spread), 0.0).astype(BF)
    output = (base + adapter_scale * mm(shrunk_wide, up_got)).astype(BF)
    input_gradient = (mm(cot, weight, 1, 1) + mm(d_wide, down_got)).astype(BF)

    s_ad = jnp.where(ad_block, mm(both_got[:, :rank], spread_ad), 0.0).astype(BF)
    d_ad = jnp.where(ad_block, mm(both_got[:, rank:], spread_ad), 0.0).astype(BF)
    grad_down = mm(d_ad, tok_got, 0, 0).astype(BF).reshape(n_own, rank, half_d)
    grad_up = (adapter_scale * mm(s_ad, cot_got, 0, 0)).astype(BF)
    return output, input_gradient, grad_down, grad_up.reshape(n_own, rank, half_out)


def solution(mesh):
    in_specs = (
        P(("groups", "dp"), "tensor"),
        P("tensor", None),
        P("dp", None, "tensor"),
        P("dp", None, None),
        P(("groups", "dp")),
        P(("groups", "dp")),
        P(("groups", "dp"), None),
    )
    out_specs = (
        P(("groups", "dp"), "tensor"),
        P(("groups", "dp"), "tensor"),
        P(("groups", "dp"), None, "tensor"),
        P(("groups", "dp"), None, "tensor"),
    )
    return jax.shard_map(local, mesh=mesh, in_specs=in_specs, out_specs=out_specs, check_vma=False)
```

```python
import functools

import jax
import jax.numpy as jnp
from jax import lax
from jax.experimental import pallas as pl
from jax.experimental.pallas import tpu as pltpu
from jax.sharding import PartitionSpec as P

adapter_scale = 2.0
BF = jnp.bfloat16
F32 = jnp.float32


def mm(a, b, ca=1, cb=0, **kw):
    return lax.dot_general(
        a, b, (((ca,), (cb,)), ((), ())), preferred_element_type=F32, **kw
    )


def local_ops(tokens, weight, down, up, index, length, cot):
    dp = lax.axis_size("dp")
    seg_dev = index.shape[0]
    rows, half_d = tokens.shape
    seg_len = rows // seg_dev
    full_out = weight.shape[1]
    half_out = full_out // lax.axis_size("tensor")
    n_own, rank = down.shape[0], down.shape[1]
    per_owner = max(1, -(-seg_dev // dp))
    n_slots = dp * per_owner
    n_tok, n_rank, n_ad = n_slots * seg_len, n_slots * rank, n_own * rank
    column = lax.axis_index("tensor") * half_out

    owners = index // n_own
    local_index = index - owners * n_own
    pos = jnp.arange(seg_dev, dtype=jnp.int32)
    earlier = (owners[:, None] == owners[None, :]) & (pos[None, :] < pos[:, None])
    placed = owners * per_owner + jnp.sum(earlier.astype(jnp.int32), axis=1)
    picker = placed[None, :] == jnp.arange(n_slots, dtype=jnp.int32)[:, None]
    request = jnp.sum(jnp.where(picker, local_index[None, :] + 1, 0), axis=1)
    requested = (
        lax.all_to_all(
            request.reshape(dp, per_owner), "dp", split_axis=0, concat_axis=0, tiled=True
        ).reshape(n_slots)
        - 1
    )

    row_i = jnp.arange(rows, dtype=jnp.int32)
    placed_row = jnp.repeat(placed, seg_len)
    dest = placed_row * seg_len + row_i % seg_len
    live = (row_i % seg_len < jnp.repeat(length, seg_len)).astype(F32)[:, None]
    tok_i = jnp.arange(n_tok, dtype=jnp.int32)
    rank_i = jnp.arange(n_rank, dtype=jnp.int32)
    ad_i = jnp.arange(n_ad, dtype=jnp.int32)
    r_i = jnp.arange(rank, dtype=jnp.int32)
    place = (tok_i[:, None] == dest[None, :]).astype(BF)
    source = jnp.repeat(requested, rank) * rank + rank_i % rank
    choose = (source[:, None] == ad_i[None, :]).astype(BF)
    own_block = placed_row[:, None] == (rank_i // rank)[None, :]
    ad_block = jnp.repeat(requested, seg_len)[:, None] == (ad_i // rank)[None, :]
    spread = (rank_i[None, :] % rank == r_i[:, None]).astype(BF)
    spread_ad = (ad_i[None, :] % rank == r_i[:, None]).astype(BF)

    def exchange(x):
        y = lax.all_to_all(
            x.reshape(dp, x.shape[0] // dp, x.shape[1]),
            "dp", split_axis=0, concat_axis=0, tiled=True,
        )
        return y.reshape(x.shape)

    cot_half = lax.dynamic_slice_in_dim(cot, column, half_out, 1)
    up2 = lax.dynamic_slice_in_dim(up.reshape(n_ad, full_out), column, half_out, 1)
    tok_got = exchange(mm(place, tokens).astype(BF))
    cot_got = exchange(mm(place, cot_half).astype(BF))
    up_got = exchange(mm(choose, up2).astype(BF))
    down_got = exchange(mm(choose, down.reshape(n_ad, half_d)).astype(BF))

    base = lax.psum_scatter(mm(tokens, weight), "tensor", scatter_dimension=1, tiled=True)

    def compact(full):
        masked = jnp.where(own_block, full, 0.0)
        return mm(masked, spread.astype(F32), 1, 1, precision=lax.Precision.HIGHEST)

    parts = jnp.concatenate(
        [compact(mm(tokens, down_got, 1, 1)), compact(mm(cot_half, up_got, 1, 1))], axis=1
    )
    sums = lax.psum(parts, "tensor") * live
    shrunk = sums[:, :rank].astype(BF)
    d_shrunk = (adapter_scale * sums[:, rank:]).astype(BF)
    both = jnp.concatenate([shrunk, d_shrunk], axis=1)
    both_got = exchange(mm(place, both).astype(BF))

    shrunk_wide = jnp.where(own_block, mm(shrunk, spread), 0.0).astype(BF)
    d_wide = jnp.where(own_block, mm(d_shrunk, spread), 0.0).astype(BF)
    output = (base + adapter_scale * mm(shrunk_wide, up_got)).astype(BF)
    input_gradient = (mm(cot, weight, 1, 1) + mm(d_wide, down_got)).astype(BF)

    s_ad = jnp.where(ad_block, mm(both_got[:, :rank], spread_ad), 0.0).astype(BF)
    d_ad = jnp.where(ad_block, mm(both_got[:, rank:], spread_ad), 0.0).astype(BF)
    grad_down = mm(d_ad, tok_got, 0, 0).astype(BF).reshape(n_own, rank, half_d)
    grad_up = (adapter_scale * mm(s_ad, cot_got, 0, 0)).astype(BF)
    return output, input_gradient, grad_down, grad_up.reshape(n_own, rank, half_out)

MESH = pl.DeviceIdType.MESH


def kernel(
    dp, per_owner, seg_len, rank, tile,
    tokens, weight, down, up, cot, dest, placed_row, live, request,
    output, input_gradient, grad_down, grad_up,
    tok_send, tok_got, ad_send, ad_got, req_got, both, both_send, both_got,
    base, base_got, part, part_got, s_full,
    req_ss, req_rs, ad_ss, ad_rs, tok_ss, tok_rs, both_ss, both_rs, core_ss, core_rs,
):
    me = lax.axis_index("dp")
    core = lax.axis_index("tensor")
    rows, half_d = tokens.shape
    n_ad = down.shape[0]
    half_out = output.shape[1]
    blk = per_owner * seg_len
    tiles = half_d // tile
    column = pl.multiple_of(core * half_out, 128)
    other = pl.multiple_of((1 - core) * half_out, 128)

    def peer(k):
        return lax.rem(me + k, dp)

    def cut(p, size=blk):
        return pl.ds(pl.multiple_of(p * size, size), size)

    def send(src, dst, ss, rs, k, size=blk):
        p = peer(k)
        return pltpu.make_async_remote_copy(
            src_ref=src.at[cut(p, size)], dst_ref=dst.at[cut(me, size)],
            send_sem=ss.at[k], recv_sem=rs.at[k],
            device_id={"dp": p}, device_id_type=MESH,
        )

    def to_core(src, dst, i):
        return pltpu.make_async_remote_copy(
            src_ref=src, dst_ref=dst, send_sem=core_ss.at[i], recv_sem=core_rs.at[i],
            device_id={"tensor": 1 - core}, device_id_type=MESH,
        )

    barrier = pltpu.get_barrier_semaphore()

    @pl.loop(1, dp)
    def _(k):
        pl.semaphore_signal(barrier, 1, device_id={"dp": peer(k)}, device_id_type=MESH)

    pl.semaphore_signal(barrier, 1, device_id={"tensor": 1 - core}, device_id_type=MESH)
    pl.semaphore_wait(barrier, dp)

    @pl.loop(1, dp)
    def _(k):
        send(request, req_got, req_ss, req_rs, k, 8).start()

    req_got[cut(me, 8)] = request[cut(me, 8)]

    def pack(p, lhs, wide, narrow, narrow_cols, dst, drow):
        @pl.loop(0, tiles)
        def _(j):
            c = pl.ds(pl.multiple_of(j * tile, tile), tile)
            dst[cut(drow), c] = mm(lhs, wide[:, c]).astype(BF)

        dst[cut(drow), half_d:] = mm(lhs, narrow[:, narrow_cols]).astype(BF)

    def place_of(p):
        i = lax.broadcasted_iota(jnp.int32, (blk, rows), 0) + p * blk
        return jnp.where(i == dest[...], 1.0, 0.0).astype(BF)

    def pack_tok(k, dst):
        p = peer(k)
        pack(p, place_of(p), tokens, cot, pl.ds(column, half_out), dst, p)

    pack_tok(0, tok_got)

    @pl.loop(1, FIRST)
    def _(i):
        k = ORDER(i, dp)
        pack_tok(k, tok_send)
        send(tok_send, tok_got, tok_ss, tok_rs, k).start()

    @pl.loop(1, dp)
    def _(k):
        send(request, req_got, req_ss, req_rs, k, 8).wait()

    def wanted(p, n):
        i = lax.broadcasted_iota(jnp.int32, (n, dp * 8), 0)
        j = lax.broadcasted_iota(jnp.int32, (n, dp * 8), 1)
        if p is None:
            hit = j == (i // blk) * 8 + (i % blk) // rank
        else:
            hit = j == p * 8 + i // rank
        return mm(jnp.where(hit, 1.0, 0.0).astype(BF), req_got[...].astype(BF))

    def pack_ad(k, dst):
        p = peer(k)
        i = lax.broadcasted_iota(jnp.int32, (blk, n_ad), 0)
        j = lax.broadcasted_iota(jnp.int32, (blk, n_ad), 1)
        source = wanted(p, blk) * float(rank) + (i % rank).astype(F32)
        lhs = jnp.where(source == j.astype(F32), 1.0, 0.0).astype(BF)
        pack(p, lhs, down, up, pl.ds(column, half_out), dst, p)

    @pl.loop(1, dp)
    def _(i):
        k = ORDER(i, dp)
        pack_ad(k, ad_send)
        send(ad_send, ad_got, ad_ss, ad_rs, k).start()

    pack_ad(0, ad_got)

    @pl.loop(FIRST, dp)
    def _(i):
        k = ORDER(i, dp)
        pack_tok(k, tok_send)
        send(tok_send, tok_got, tok_ss, tok_rs, k).start()

    base[...] = jnp.zeros_like(base)

    @pl.loop(0, tiles)
    def _(j):
        c = pl.ds(pl.multiple_of(j * tile, tile), tile)
        base[0] += mm(tokens[:, c], weight[c, pl.ds(column, half_out)])
        base[1] += mm(tokens[:, c], weight[c, pl.ds(other, half_out)])

    swap_base = to_core(base.at[1], base_got, 0)
    swap_base.start()

    @pl.loop(1, dp)
    def _(k):
        send(ad_send, ad_got, ad_ss, ad_rs, k).wait()

    n_rank = ad_got.shape[0]
    own_block = placed_row[...] == lax.broadcasted_iota(jnp.int32, (rows, n_rank), 1) // rank
    s_full[...] = jnp.zeros_like(s_full)

    @pl.loop(0, tiles)
    def _(j):
        c = pl.ds(pl.multiple_of(j * tile, tile), tile)
        s_full[...] += mm(tokens[:, c], ad_got[:, c], 1, 1)

    def lane_map(shape, lane_axis, shift):
        lane = lax.broadcasted_iota(jnp.int32, shape, lane_axis)
        i = lax.broadcasted_iota(jnp.int32, shape, 1 - lane_axis)
        return jnp.where(lane == i % rank + shift, 1.0, 0.0)

    def compact(full, shift):
        return mm(
            jnp.where(own_block, full, 0.0), lane_map((n_rank, 128), 1, shift),
            precision=lax.Precision.HIGHEST,
        )

    t_full = mm(cot[:, pl.ds(column, half_out)], ad_got[:, half_d:], 1, 1)
    part[...] = compact(s_full[...], 0) + compact(t_full, rank)
    swap_part = to_core(part, part_got, 1)
    swap_part.start()
    swap_part.wait()
    lanes = lax.broadcasted_iota(jnp.int32, part.shape, 1)
    factor = jnp.where(lanes < rank, 1.0, adapter_scale) * live[...]
    both[...] = ((part[...] + part_got[...]) * factor).astype(BF)

    @pl.loop(1, dp)
    def _(k):
        p = peer(k)
        both_send[cut(p)] = mm(place_of(p), both[...]).astype(BF)
        send(both_send, both_got, both_ss, both_rs, k).start()

    both_got[cut(me)] = mm(place_of(me), both[...]).astype(BF)

    def widen(shift):
        wide = mm(both[...], lane_map((128, n_rank), 0, shift).astype(BF))
        return jnp.where(own_block, wide, 0.0).astype(BF)

    shrunk_wide = widen(0)
    d_wide = widen(rank)
    swap_base.wait()
    extra = mm(shrunk_wide, ad_got[:, half_d:])
    output[...] = (base[0] + base_got[...] + adapter_scale * extra).astype(BF)

    @pl.loop(0, tiles)
    def _(j):
        c = pl.ds(pl.multiple_of(j * tile, tile), tile)
        frozen = mm(cot[...], weight[c, :], 1, 1)
        input_gradient[:, c] = (frozen + mm(d_wide, ad_got[:, c])).astype(BF)

    @pl.loop(1, dp)
    def _(k):
        send(both_send, both_got, both_ss, both_rs, k).wait()

    n_tok = tok_got.shape[0]
    ad_i = lax.broadcasted_iota(jnp.int32, (n_tok, n_ad), 1) // rank
    ad_block = wanted(None, n_tok) == ad_i.astype(F32)

    def widen_ad(shift):
        wide = mm(both_got[...], lane_map((128, n_ad), 0, shift).astype(BF))
        return jnp.where(ad_block, wide, 0.0).T.astype(BF)

    s_ad = widen_ad(0)
    d_ad = widen_ad(rank)

    @pl.loop(1, dp)
    def _(k):
        send(tok_send, tok_got, tok_ss, tok_rs, k).wait()

    @pl.loop(0, tiles)
    def _(j):
        c = pl.ds(pl.multiple_of(j * tile, tile), tile)
        grad_down[:, c] = mm(d_ad, tok_got[:, c]).astype(BF)

    grad_up[...] = (adapter_scale * mm(s_ad, tok_got[:, half_d:])).astype(BF)


FIRST = 3


def ORDER(i, dp):
    return lax.rem(i + dp // 2 - 2, dp - 1) + 1


def local(tokens, weight, down, up, index, length, cot):
    dp = lax.axis_size("dp")
    seg_dev = index.shape[0]
    rows, half_d = tokens.shape
    seg_len = rows // seg_dev
    n_own, rank, full_out = up.shape
    half_out = full_out // lax.axis_size("tensor")
    per_owner = max(1, -(-seg_dev // dp))
    n_ad = n_own * rank
    if dp * per_owner != seg_dev or per_owner > 8 or rank != seg_len or n_ad % 128 or n_own > 256:
        return local_ops(tokens, weight, down, up, index, length, cot)
    owners = index // n_own
    local_index = index - owners * n_own
    pos = jnp.arange(seg_dev, dtype=jnp.int32)
    earlier = (owners[:, None] == owners[None, :]) & (pos[None, :] < pos[:, None])
    placed = owners * per_owner + jnp.sum(earlier.astype(jnp.int32), axis=1)
    slot8 = placed // per_owner * 8 + placed % per_owner
    hit = slot8[None, :] == jnp.arange(dp * 8, dtype=jnp.int32)[:, None]
    request = jnp.sum(jnp.where(hit, local_index[None, :] + 1, 0), axis=1) - 1
    request = jnp.broadcast_to(request.astype(F32)[:, None], (dp * 8, n_ad))
    row_i = jnp.arange(rows, dtype=jnp.int32)
    placed_row = jnp.repeat(placed, seg_len)
    dest = (placed_row * seg_len + row_i % seg_len)[None, :]
    live = (row_i % seg_len < jnp.repeat(length, seg_len)).astype(F32)[:, None]
    wide = half_d + half_out
    tile = 512 if half_d % 512 == 0 else 128
    vmem = pl.BlockSpec(memory_space=pltpu.VMEM)
    dma = pltpu.SemaphoreType.DMA((dp,))
    outs = pl.pallas_call(
        functools.partial(kernel, dp, per_owner, seg_len, rank, tile),
        out_shape=[
            jax.ShapeDtypeStruct((rows, half_out), BF),
            jax.ShapeDtypeStruct((rows, half_d), BF),
            jax.ShapeDtypeStruct((n_ad, half_d), BF),
            jax.ShapeDtypeStruct((n_ad, half_out), BF),
        ],
        in_specs=[vmem] * 9,
        out_specs=[vmem] * 4,
        scratch_shapes=[
            pltpu.VMEM((rows, wide), BF),
            pltpu.VMEM((rows, wide), BF),
            pltpu.VMEM((rows, wide), BF),
            pltpu.VMEM((rows, wide), BF),
            pltpu.VMEM((dp * 8, n_ad), F32),
            pltpu.VMEM((rows, 128), BF),
            pltpu.VMEM((rows, 128), BF),
            pltpu.VMEM((rows, 128), BF),
            pltpu.VMEM((2, rows, half_out), F32),
            pltpu.VMEM((rows, half_out), F32),
            pltpu.VMEM((rows, 128), F32),
            pltpu.VMEM((rows, 128), F32),
            pltpu.VMEM((rows, rows), F32),
            dma, dma, dma, dma, dma, dma, dma, dma,
            pltpu.SemaphoreType.DMA((2,)),
            pltpu.SemaphoreType.DMA((2,)),
        ],
        compiler_params=pltpu.CompilerParams(
            collective_id=0, has_side_effects=True, vmem_limit_bytes=56 * 2**20
        ),
        cost_estimate=pl.CostEstimate(
            flops=8 * rows * half_d * full_out, bytes_accessed=16 * rows * half_d, transcendentals=0
        ),
    )(
        tokens, weight, down.reshape(n_ad, half_d), up.reshape(n_ad, full_out),
        cot, dest, placed_row[:, None], live, request,
    )
    output, input_gradient, grad_down, grad_up = outs
    return (
        output, input_gradient,
        grad_down.reshape(n_own, rank, half_d), grad_up.reshape(n_own, rank, half_out),
    )


def solution(mesh):
    in_specs = (
        P(("groups", "dp"), "tensor"),
        P("tensor", None),
        P("dp", None, "tensor"),
        P("dp", None, None),
        P(("groups", "dp")),
        P(("groups", "dp")),
        P(("groups", "dp"), None),
    )
    out_specs = (
        P(("groups", "dp"), "tensor"),
        P(("groups", "dp"), "tensor"),
        P(("groups", "dp"), None, "tensor"),
        P(("groups", "dp"), None, "tensor"),
    )
    return jax.shard_map(local, mesh=mesh, in_specs=in_specs, out_specs=out_specs, check_vma=False)
```

```python
import functools

import jax
import jax.numpy as jnp
from jax import lax
from jax.experimental import pallas as pl
from jax.experimental.pallas import tpu as pltpu
from jax.sharding import PartitionSpec as P

adapter_scale = 2.0
BF = jnp.bfloat16
F32 = jnp.float32


def mm(a, b, ca=1, cb=0, **kw):
    return lax.dot_general(
        a, b, (((ca,), (cb,)), ((), ())), preferred_element_type=F32, **kw
    )


def local_ops(tokens, weight, down, up, index, length, cot):
    dp = lax.axis_size("dp")
    seg_dev = index.shape[0]
    rows, half_d = tokens.shape
    seg_len = rows // seg_dev
    full_out = weight.shape[1]
    half_out = full_out // lax.axis_size("tensor")
    n_own, rank = down.shape[0], down.shape[1]
    per_owner = max(1, -(-seg_dev // dp))
    n_slots = dp * per_owner
    n_tok, n_rank, n_ad = n_slots * seg_len, n_slots * rank, n_own * rank
    column = lax.axis_index("tensor") * half_out

    owners = index // n_own
    local_index = index - owners * n_own
    pos = jnp.arange(seg_dev, dtype=jnp.int32)
    earlier = (owners[:, None] == owners[None, :]) & (pos[None, :] < pos[:, None])
    placed = owners * per_owner + jnp.sum(earlier.astype(jnp.int32), axis=1)
    picker = placed[None, :] == jnp.arange(n_slots, dtype=jnp.int32)[:, None]
    request = jnp.sum(jnp.where(picker, local_index[None, :] + 1, 0), axis=1)
    requested = (
        lax.all_to_all(
            request.reshape(dp, per_owner), "dp", split_axis=0, concat_axis=0, tiled=True
        ).reshape(n_slots)
        - 1
    )

    row_i = jnp.arange(rows, dtype=jnp.int32)
    placed_row = jnp.repeat(placed, seg_len)
    dest = placed_row * seg_len + row_i % seg_len
    live = (row_i % seg_len < jnp.repeat(length, seg_len)).astype(F32)[:, None]
    tok_i = jnp.arange(n_tok, dtype=jnp.int32)
    rank_i = jnp.arange(n_rank, dtype=jnp.int32)
    ad_i = jnp.arange(n_ad, dtype=jnp.int32)
    r_i = jnp.arange(rank, dtype=jnp.int32)
    place = (tok_i[:, None] == dest[None, :]).astype(BF)
    source = jnp.repeat(requested, rank) * rank + rank_i % rank
    choose = (source[:, None] == ad_i[None, :]).astype(BF)
    own_block = placed_row[:, None] == (rank_i // rank)[None, :]
    ad_block = jnp.repeat(requested, seg_len)[:, None] == (ad_i // rank)[None, :]
    spread = (rank_i[None, :] % rank == r_i[:, None]).astype(BF)
    spread_ad = (ad_i[None, :] % rank == r_i[:, None]).astype(BF)

    def exchange(x):
        y = lax.all_to_all(
            x.reshape(dp, x.shape[0] // dp, x.shape[1]),
            "dp", split_axis=0, concat_axis=0, tiled=True,
        )
        return y.reshape(x.shape)

    cot_half = lax.dynamic_slice_in_dim(cot, column, half_out, 1)
    up2 = lax.dynamic_slice_in_dim(up.reshape(n_ad, full_out), column, half_out, 1)
    tok_got = exchange(mm(place, tokens).astype(BF))
    cot_got = exchange(mm(place, cot_half).astype(BF))
    up_got = exchange(mm(choose, up2).astype(BF))
    down_got = exchange(mm(choose, down.reshape(n_ad, half_d)).astype(BF))

    base = lax.psum_scatter(mm(tokens, weight), "tensor", scatter_dimension=1, tiled=True)

    def compact(full):
        masked = jnp.where(own_block, full, 0.0)
        return mm(masked, spread.astype(F32), 1, 1, precision=lax.Precision.HIGHEST)

    parts = jnp.concatenate(
        [compact(mm(tokens, down_got, 1, 1)), compact(mm(cot_half, up_got, 1, 1))], axis=1
    )
    sums = lax.psum(parts, "tensor") * live
    shrunk = sums[:, :rank].astype(BF)
    d_shrunk = (adapter_scale * sums[:, rank:]).astype(BF)
    both = jnp.concatenate([shrunk, d_shrunk], axis=1)
    both_got = exchange(mm(place, both).astype(BF))

    shrunk_wide = jnp.where(own_block, mm(shrunk, spread), 0.0).astype(BF)
    d_wide = jnp.where(own_block, mm(d_shrunk, spread), 0.0).astype(BF)
    output = (base + adapter_scale * mm(shrunk_wide, up_got)).astype(BF)
    input_gradient = (mm(cot, weight, 1, 1) + mm(d_wide, down_got)).astype(BF)

    s_ad = jnp.where(ad_block, mm(both_got[:, :rank], spread_ad), 0.0).astype(BF)
    d_ad = jnp.where(ad_block, mm(both_got[:, rank:], spread_ad), 0.0).astype(BF)
    grad_down = mm(d_ad, tok_got, 0, 0).astype(BF).reshape(n_own, rank, half_d)
    grad_up = (adapter_scale * mm(s_ad, cot_got, 0, 0)).astype(BF)
    return output, input_gradient, grad_down, grad_up.reshape(n_own, rank, half_out)

MESH = pl.DeviceIdType.MESH


def kernel(
    dp, per_owner, seg_len, rank, tile,
    tokens, weight, down, up, cot, dest, placed_row, live, request,
    output, input_gradient, grad_down, grad_up,
    tok_send, tok_got, ad_send, ad_got, req_got, both, both_send, both_got,
    base, base_got, part, part_got, s_full, mirror, req_far,
    req_ss, req_rs, ad_ss, ad_rs, tok_ss, tok_rs, both_ss, both_rs, core_ss, core_rs,
    mir_ss, mir_rs, far_ss, far_rs, x_ss, x_rs, reqf_ss, reqf_rs,
):
    me = lax.axis_index("dp")
    core = lax.axis_index("tensor")
    group = lax.axis_index("groups")
    half = dp // 2
    first = me // half * half
    opposite = lax.rem(me + half, dp)
    rows, half_d = tokens.shape
    n_ad = down.shape[0]
    half_out = output.shape[1]
    blk = per_owner * seg_len
    tiles = half_d // tile
    column = pl.multiple_of(core * half_out, 128)
    other = pl.multiple_of((1 - core) * half_out, 128)

    def peer(k):
        return lax.rem(me + k, dp)

    def near(j):
        return first + lax.rem(me - first + j, half)

    def far(p):
        return lax.rem(p + half, dp)

    def step(p):
        return lax.rem(p - me + dp, dp)

    def cut(p, size=blk):
        return pl.ds(pl.multiple_of(p * size, size), size)

    def send(src, dst, ss, rs, k, size=blk):
        p = peer(k)
        return pltpu.make_async_remote_copy(
            src_ref=src.at[cut(p, size)], dst_ref=dst.at[cut(me, size)],
            send_sem=ss.at[k], recv_sem=rs.at[k],
            device_id={"dp": p}, device_id_type=MESH,
        )

    def to_core(src, dst, i):
        return pltpu.make_async_remote_copy(
            src_ref=src, dst_ref=dst, send_sem=core_ss.at[i], recv_sem=core_rs.at[i],
            device_id={"tensor": 1 - core}, device_id_type=MESH,
        )

    def to_near(src, dst, from_part, to_part, ss, rs, j, size=blk):
        return pltpu.make_async_remote_copy(
            src_ref=src.at[cut(from_part, size)], dst_ref=dst.at[cut(to_part, size)],
            send_sem=ss.at[j], recv_sem=rs.at[j],
            device_id={"dp": near(j)}, device_id_type=MESH,
        )

    def own_ad(j):
        return to_near(ad_send, ad_got, near(j), me, ad_ss, ad_rs, j)

    def mirror_ad(j):
        return to_near(ad_send, ad_got, far(near(j)), opposite, far_ss, far_rs, j)

    def far_request(j):
        return to_near(request, req_far, far(near(j)), me, reqf_ss, reqf_rs, j, 8)

    piece = n_ad // 2 // PIECES

    def piece_rows(c):
        return pl.ds(pl.multiple_of((group * PIECES + c) * piece, piece), piece)

    def across(c, which):
        r = piece_rows(c)
        src = down.at[r] if which == 0 else up.at[r, pl.ds(column, half_out)]
        cols = pl.ds(0, half_d) if which == 0 else pl.ds(half_d, half_out)
        return pltpu.make_async_remote_copy(
            src_ref=src, dst_ref=mirror.at[r, cols],
            send_sem=mir_ss.at[which, c], recv_sem=mir_rs.at[which, c],
            device_id={"dp": opposite}, device_id_type=MESH,
        )

    def share(c):
        r = piece_rows(c)
        return pltpu.make_async_remote_copy(
            src_ref=mirror.at[r], dst_ref=mirror.at[r],
            send_sem=x_ss.at[c], recv_sem=x_rs.at[c],
            device_id={"groups": 1 - group}, device_id_type=MESH,
        )

    req_far[...] = jnp.zeros_like(req_far)
    barrier = pltpu.get_barrier_semaphore()

    @pl.loop(1, dp)
    def _(k):
        pl.semaphore_signal(barrier, 1, device_id={"dp": peer(k)}, device_id_type=MESH)

    pl.semaphore_signal(barrier, 1, device_id={"tensor": 1 - core}, device_id_type=MESH)
    pl.semaphore_signal(barrier, 1, device_id={"groups": 1 - group}, device_id_type=MESH)
    pl.semaphore_wait(barrier, dp + 1)

    @pl.loop(1, dp)
    def _(k):
        send(request, req_got, req_ss, req_rs, k, 8).start()

    @pl.loop(1, half)
    def _(j):
        far_request(j).start()

    @pl.loop(0, PIECES)
    def _(c):
        across(c, 0).start()
        across(c, 1).start()

    req_got[cut(me, 8)] = request[cut(me, 8)]
    req_far[cut(me, 8)] = request[cut(opposite, 8)]

    def pack(lhs, wide, narrow, narrow_cols, dst, drow):
        @pl.loop(0, tiles)
        def _(j):
            c = pl.ds(pl.multiple_of(j * tile, tile), tile)
            dst[cut(drow), c] = mm(lhs, wide[:, c]).astype(BF)

        dst[cut(drow), half_d:] = mm(lhs, narrow[:, narrow_cols]).astype(BF)

    def place_of(p):
        i = lax.broadcasted_iota(jnp.int32, (blk, rows), 0) + p * blk
        return jnp.where(i == dest[...], 1.0, 0.0).astype(BF)

    def pack_tok(k, dst):
        p = peer(k)
        pack(place_of(p), tokens, cot, pl.ds(column, half_out), dst, p)

    @pl.loop(1, half)
    def _(j):
        k = step(near(j))
        pack_tok(k, tok_send)
        send(tok_send, tok_got, tok_ss, tok_rs, k).start()

    @pl.loop(1, dp)
    def _(k):
        send(request, req_got, req_ss, req_rs, k, 8).wait()

    @pl.loop(1, half)
    def _(j):
        far_request(j).wait()

    def wanted(p, n, req_got=req_got):
        i = lax.broadcasted_iota(jnp.int32, (n, dp * 8), 0)
        j = lax.broadcasted_iota(jnp.int32, (n, dp * 8), 1)
        if p is None:
            hit = j == (i // blk) * 8 + (i % blk) // rank
        else:
            hit = j == p * 8 + i // rank
        return mm(jnp.where(hit, 1.0, 0.0).astype(BF), req_got[...].astype(BF))

    def pack_ad(p, req, wide, narrow, narrow_cols, dst, drow):
        i = lax.broadcasted_iota(jnp.int32, (blk, n_ad), 0)
        j = lax.broadcasted_iota(jnp.int32, (blk, n_ad), 1)
        source = wanted(p, blk, req) * float(rank) + (i % rank).astype(F32)
        lhs = jnp.where(source == j.astype(F32), 1.0, 0.0).astype(BF)
        pack(lhs, wide, narrow, narrow_cols, dst, drow)

    def pack_own(p, dst, drow):
        pack_ad(p, req_got, down, up, pl.ds(column, half_out), dst, drow)

    def pack_mirror(p, dst, drow):
        pack_ad(p, req_far, mirror, mirror, pl.ds(half_d, half_out), dst, drow)

    @pl.loop(1, half)
    def _(j):
        pack_own(near(j), ad_send, near(j))
        own_ad(j).start()

    def far_tok(j):
        return send(tok_send, tok_got, tok_ss, tok_rs, step(far(near(j))))

    @pl.loop(0, half)
    def _(j):
        pack_tok(step(far(near(j))), tok_send)

    @pl.loop(0, EARLY)
    def _(j):
        far_tok(j).start()

    pack_tok(0, tok_got)
    pack_own(me, ad_got, me)

    base[...] = jnp.zeros_like(base)

    @pl.loop(0, tiles)
    def _(j):
        c = pl.ds(pl.multiple_of(j * tile, tile), tile)
        base[0] += mm(tokens[:, c], weight[c, pl.ds(column, half_out)])
        base[1] += mm(tokens[:, c], weight[c, pl.ds(other, half_out)])

    swap_base = to_core(base.at[1], base_got, 0)
    swap_base.start()

    @pl.loop(0, PIECES)
    def _(c):
        across(c, 0).wait()
        across(c, 1).wait()
        share(c).start()

    @pl.loop(EARLY, half)
    def _(j):
        far_tok(j).start()

    @pl.loop(0, PIECES)
    def _(c):
        share(c).wait()

    @pl.loop(1, half)
    def _(j):
        pack_mirror(near(j), ad_send, far(near(j)))
        mirror_ad(j).start()

    pack_mirror(me, ad_got, opposite)

    @pl.loop(1, half)
    def _(j):
        own_ad(j).wait()

    @pl.loop(1, half)
    def _(j):
        mirror_ad(j).wait()

    n_rank = ad_got.shape[0]
    own_block = placed_row[...] == lax.broadcasted_iota(jnp.int32, (rows, n_rank), 1) // rank
    s_full[...] = jnp.zeros_like(s_full)

    @pl.loop(0, tiles)
    def _(j):
        c = pl.ds(pl.multiple_of(j * tile, tile), tile)
        s_full[...] += mm(tokens[:, c], ad_got[:, c], 1, 1)

    def lane_map(shape, lane_axis, shift):
        lane = lax.broadcasted_iota(jnp.int32, shape, lane_axis)
        i = lax.broadcasted_iota(jnp.int32, shape, 1 - lane_axis)
        return jnp.where(lane == i % rank + shift, 1.0, 0.0)

    def compact(full, shift):
        return mm(
            jnp.where(own_block, full, 0.0), lane_map((n_rank, 128), 1, shift),
            precision=lax.Precision.HIGHEST,
        )

    t_full = mm(cot[:, pl.ds(column, half_out)], ad_got[:, half_d:], 1, 1)
    part[...] = compact(s_full[...], 0) + compact(t_full, rank)
    swap_part = to_core(part, part_got, 1)
    swap_part.start()
    swap_part.wait()
    lanes = lax.broadcasted_iota(jnp.int32, part.shape, 1)
    factor = jnp.where(lanes < rank, 1.0, adapter_scale) * live[...]
    both[...] = ((part[...] + part_got[...]) * factor).astype(BF)

    @pl.loop(1, dp)
    def _(k):
        p = peer(k)
        both_send[cut(p)] = mm(place_of(p), both[...]).astype(BF)
        send(both_send, both_got, both_ss, both_rs, k).start()

    both_got[cut(me)] = mm(place_of(me), both[...]).astype(BF)

    def widen(shift):
        wide = mm(both[...], lane_map((128, n_rank), 0, shift).astype(BF))
        return jnp.where(own_block, wide, 0.0).astype(BF)

    shrunk_wide = widen(0)
    d_wide = widen(rank)
    swap_base.wait()
    extra = mm(shrunk_wide, ad_got[:, half_d:])
    output[...] = (base[0] + base_got[...] + adapter_scale * extra).astype(BF)

    @pl.loop(0, tiles)
    def _(j):
        c = pl.ds(pl.multiple_of(j * tile, tile), tile)
        frozen = mm(cot[...], weight[c, :], 1, 1)
        input_gradient[:, c] = (frozen + mm(d_wide, ad_got[:, c])).astype(BF)

    @pl.loop(1, dp)
    def _(k):
        send(both_send, both_got, both_ss, both_rs, k).wait()

    n_tok = tok_got.shape[0]
    ad_i = lax.broadcasted_iota(jnp.int32, (n_tok, n_ad), 1) // rank
    ad_block = wanted(None, n_tok) == ad_i.astype(F32)

    def widen_ad(shift):
        wide = mm(both_got[...], lane_map((128, n_ad), 0, shift).astype(BF))
        return jnp.where(ad_block, wide, 0.0).T.astype(BF)

    s_ad = widen_ad(0)
    d_ad = widen_ad(rank)

    @pl.loop(1, dp)
    def _(k):
        send(tok_send, tok_got, tok_ss, tok_rs, k).wait()

    @pl.loop(0, tiles)
    def _(j):
        c = pl.ds(pl.multiple_of(j * tile, tile), tile)
        grad_down[:, c] = mm(d_ad, tok_got[:, c]).astype(BF)

    grad_up[...] = (adapter_scale * mm(s_ad, tok_got[:, half_d:])).astype(BF)


PIECES = 4
EARLY = 1


def local(tokens, weight, down, up, index, length, cot):
    dp = lax.axis_size("dp")
    seg_dev = index.shape[0]
    rows, half_d = tokens.shape
    seg_len = rows // seg_dev
    n_own, rank, full_out = up.shape
    half_out = full_out // lax.axis_size("tensor")
    per_owner = max(1, -(-seg_dev // dp))
    n_ad = n_own * rank
    if dp * per_owner != seg_dev or per_owner > 8 or rank != seg_len or n_ad % 128 or n_own > 256 or n_ad % (32 * PIECES) or dp % 2 or lax.axis_size("groups") != 2:
        return local_ops(tokens, weight, down, up, index, length, cot)
    owners = index // n_own
    local_index = index - owners * n_own
    pos = jnp.arange(seg_dev, dtype=jnp.int32)
    earlier = (owners[:, None] == owners[None, :]) & (pos[None, :] < pos[:, None])
    placed = owners * per_owner + jnp.sum(earlier.astype(jnp.int32), axis=1)
    slot8 = placed // per_owner * 8 + placed % per_owner
    hit = slot8[None, :] == jnp.arange(dp * 8, dtype=jnp.int32)[:, None]
    request = jnp.sum(jnp.where(hit, local_index[None, :] + 1, 0), axis=1) - 1
    request = jnp.broadcast_to(request.astype(F32)[:, None], (dp * 8, n_ad))
    row_i = jnp.arange(rows, dtype=jnp.int32)
    placed_row = jnp.repeat(placed, seg_len)
    dest = (placed_row * seg_len + row_i % seg_len)[None, :]
    live = (row_i % seg_len < jnp.repeat(length, seg_len)).astype(F32)[:, None]
    wide = half_d + half_out
    tile = 512 if half_d % 512 == 0 else 128
    vmem = pl.BlockSpec(memory_space=pltpu.VMEM)
    dma = pltpu.SemaphoreType.DMA((dp,))
    outs = pl.pallas_call(
        functools.partial(kernel, dp, per_owner, seg_len, rank, tile),
        out_shape=[
            jax.ShapeDtypeStruct((rows, half_out), BF),
            jax.ShapeDtypeStruct((rows, half_d), BF),
            jax.ShapeDtypeStruct((n_ad, half_d), BF),
            jax.ShapeDtypeStruct((n_ad, half_out), BF),
        ],
        in_specs=[vmem] * 9,
        out_specs=[vmem] * 4,
        scratch_shapes=[
            pltpu.VMEM((rows, wide), BF),
            pltpu.VMEM((rows, wide), BF),
            pltpu.VMEM((rows, wide), BF),
            pltpu.VMEM((rows, wide), BF),
            pltpu.VMEM((dp * 8, n_ad), F32),
            pltpu.VMEM((rows, 128), BF),
            pltpu.VMEM((rows, 128), BF),
            pltpu.VMEM((rows, 128), BF),
            pltpu.VMEM((2, rows, half_out), F32),
            pltpu.VMEM((rows, half_out), F32),
            pltpu.VMEM((rows, 128), F32),
            pltpu.VMEM((rows, 128), F32),
            pltpu.VMEM((rows, rows), F32),
            pltpu.VMEM((n_ad, wide), BF),
            pltpu.VMEM((dp * 8, n_ad), F32),
            dma, dma, dma, dma, dma, dma, dma, dma,
            pltpu.SemaphoreType.DMA((2,)),
            pltpu.SemaphoreType.DMA((2,)),
            pltpu.SemaphoreType.DMA((2, PIECES)),
            pltpu.SemaphoreType.DMA((2, PIECES)),
            dma, dma,
            pltpu.SemaphoreType.DMA((PIECES,)),
            pltpu.SemaphoreType.DMA((PIECES,)),
            dma, dma,
        ],
        compiler_params=pltpu.CompilerParams(
            collective_id=0, has_side_effects=True, vmem_limit_bytes=56 * 2**20
        ),
        cost_estimate=pl.CostEstimate(
            flops=8 * rows * half_d * full_out, bytes_accessed=16 * rows * half_d, transcendentals=0
        ),
    )(
        tokens, weight, down.reshape(n_ad, half_d), up.reshape(n_ad, full_out),
        cot, dest, placed_row[:, None], live, request,
    )
    output, input_gradient, grad_down, grad_up = outs
    return (
        output, input_gradient,
        grad_down.reshape(n_own, rank, half_d), grad_up.reshape(n_own, rank, half_out),
    )


def solution(mesh):
    in_specs = (
        P(("groups", "dp"), "tensor"),
        P("tensor", None),
        P("dp", None, "tensor"),
        P("dp", None, None),
        P(("groups", "dp")),
        P(("groups", "dp")),
        P(("groups", "dp"), None),
    )
    out_specs = (
        P(("groups", "dp"), "tensor"),
        P(("groups", "dp"), "tensor"),
        P(("groups", "dp"), None, "tensor"),
        P(("groups", "dp"), None, "tensor"),
    )
    return jax.shard_map(local, mesh=mesh, in_specs=in_specs, out_specs=out_specs, check_vma=False)
```

```python
import functools

import jax
import jax.numpy as jnp
from jax import lax
from jax.experimental import pallas as pl
from jax.experimental.pallas import tpu as pltpu
from jax.sharding import PartitionSpec as P

adapter_scale = 2.0
BF = jnp.bfloat16
F32 = jnp.float32


def mm(a, b, ca=1, cb=0, **kw):
    return lax.dot_general(
        a, b, (((ca,), (cb,)), ((), ())), preferred_element_type=F32, **kw
    )


def local_ops(tokens, weight, down, up, index, length, cot):
    dp = lax.axis_size("dp")
    seg_dev = index.shape[0]
    rows, half_d = tokens.shape
    seg_len = rows // seg_dev
    full_out = weight.shape[1]
    half_out = full_out // lax.axis_size("tensor")
    n_own, rank = down.shape[0], down.shape[1]
    per_owner = max(1, -(-seg_dev // dp))
    n_slots = dp * per_owner
    n_tok, n_rank, n_ad = n_slots * seg_len, n_slots * rank, n_own * rank
    column = lax.axis_index("tensor") * half_out

    owners = index // n_own
    local_index = index - owners * n_own
    pos = jnp.arange(seg_dev, dtype=jnp.int32)
    earlier = (owners[:, None] == owners[None, :]) & (pos[None, :] < pos[:, None])
    placed = owners * per_owner + jnp.sum(earlier.astype(jnp.int32), axis=1)
    picker = placed[None, :] == jnp.arange(n_slots, dtype=jnp.int32)[:, None]
    request = jnp.sum(jnp.where(picker, local_index[None, :] + 1, 0), axis=1)
    requested = (
        lax.all_to_all(
            request.reshape(dp, per_owner), "dp", split_axis=0, concat_axis=0, tiled=True
        ).reshape(n_slots)
        - 1
    )

    row_i = jnp.arange(rows, dtype=jnp.int32)
    placed_row = jnp.repeat(placed, seg_len)
    dest = placed_row * seg_len + row_i % seg_len
    live = (row_i % seg_len < jnp.repeat(length, seg_len)).astype(F32)[:, None]
    tok_i = jnp.arange(n_tok, dtype=jnp.int32)
    rank_i = jnp.arange(n_rank, dtype=jnp.int32)
    ad_i = jnp.arange(n_ad, dtype=jnp.int32)
    r_i = jnp.arange(rank, dtype=jnp.int32)
    place = (tok_i[:, None] == dest[None, :]).astype(BF)
    source = jnp.repeat(requested, rank) * rank + rank_i % rank
    choose = (source[:, None] == ad_i[None, :]).astype(BF)
    own_block = placed_row[:, None] == (rank_i // rank)[None, :]
    ad_block = jnp.repeat(requested, seg_len)[:, None] == (ad_i // rank)[None, :]
    spread = (rank_i[None, :] % rank == r_i[:, None]).astype(BF)
    spread_ad = (ad_i[None, :] % rank == r_i[:, None]).astype(BF)

    def exchange(x):
        y = lax.all_to_all(
            x.reshape(dp, x.shape[0] // dp, x.shape[1]),
            "dp", split_axis=0, concat_axis=0, tiled=True,
        )
        return y.reshape(x.shape)

    cot_half = lax.dynamic_slice_in_dim(cot, column, half_out, 1)
    up2 = lax.dynamic_slice_in_dim(up.reshape(n_ad, full_out), column, half_out, 1)
    tok_got = exchange(mm(place, tokens).astype(BF))
    cot_got = exchange(mm(place, cot_half).astype(BF))
    up_got = exchange(mm(choose, up2).astype(BF))
    down_got = exchange(mm(choose, down.reshape(n_ad, half_d)).astype(BF))

    base = lax.psum_scatter(mm(tokens, weight), "tensor", scatter_dimension=1, tiled=True)

    def compact(full):
        masked = jnp.where(own_block, full, 0.0)
        return mm(masked, spread.astype(F32), 1, 1, precision=lax.Precision.HIGHEST)

    parts = jnp.concatenate(
        [compact(mm(tokens, down_got, 1, 1)), compact(mm(cot_half, up_got, 1, 1))], axis=1
    )
    sums = lax.psum(parts, "tensor") * live
    shrunk = sums[:, :rank].astype(BF)
    d_shrunk = (adapter_scale * sums[:, rank:]).astype(BF)
    both = jnp.concatenate([shrunk, d_shrunk], axis=1)
    both_got = exchange(mm(place, both).astype(BF))

    shrunk_wide = jnp.where(own_block, mm(shrunk, spread), 0.0).astype(BF)
    d_wide = jnp.where(own_block, mm(d_shrunk, spread), 0.0).astype(BF)
    output = (base + adapter_scale * mm(shrunk_wide, up_got)).astype(BF)
    input_gradient = (mm(cot, weight, 1, 1) + mm(d_wide, down_got)).astype(BF)

    s_ad = jnp.where(ad_block, mm(both_got[:, :rank], spread_ad), 0.0).astype(BF)
    d_ad = jnp.where(ad_block, mm(both_got[:, rank:], spread_ad), 0.0).astype(BF)
    grad_down = mm(d_ad, tok_got, 0, 0).astype(BF).reshape(n_own, rank, half_d)
    grad_up = (adapter_scale * mm(s_ad, cot_got, 0, 0)).astype(BF)
    return output, input_gradient, grad_down, grad_up.reshape(n_own, rank, half_out)

MESH = pl.DeviceIdType.MESH


def kernel(
    dp, per_owner, seg_len, rank, tile,
    tokens, weight, down, up, cot, dest, placed_row, live, request,
    output, input_gradient, grad_down, grad_up,
    tok_send, tok_got, ad_send, ad_got, req_got, both, both_send, both_got,
    base, base_got, part, part_got, s_full, mirror, req_far, frozen,
    req_ss, req_rs, ad_ss, ad_rs, tok_ss, tok_rs, both_ss, both_rs, core_ss, core_rs,
    mir_ss, mir_rs, far_ss, far_rs, x_ss, x_rs, reqf_ss, reqf_rs,
):
    me = lax.axis_index("dp")
    core = lax.axis_index("tensor")
    group = lax.axis_index("groups")
    half = dp // 2
    first = me // half * half
    opposite = lax.rem(me + half, dp)
    rows, half_d = tokens.shape
    n_ad = down.shape[0]
    half_out = output.shape[1]
    blk = per_owner * seg_len
    tiles = half_d // tile
    column = pl.multiple_of(core * half_out, 128)
    other = pl.multiple_of((1 - core) * half_out, 128)

    def peer(k):
        return lax.rem(me + k, dp)

    def near(j):
        return first + lax.rem(me - first + j, half)

    def far(p):
        return lax.rem(p + half, dp)

    def step(p):
        return lax.rem(p - me + dp, dp)

    def cut(p, size=blk):
        return pl.ds(pl.multiple_of(p * size, size), size)

    def send(src, dst, ss, rs, k, size=blk):
        p = peer(k)
        return pltpu.make_async_remote_copy(
            src_ref=src.at[cut(p, size)], dst_ref=dst.at[cut(me, size)],
            send_sem=ss.at[k], recv_sem=rs.at[k],
            device_id={"dp": p}, device_id_type=MESH,
        )

    def to_core(src, dst, i):
        return pltpu.make_async_remote_copy(
            src_ref=src, dst_ref=dst, send_sem=core_ss.at[i], recv_sem=core_rs.at[i],
            device_id={"tensor": 1 - core}, device_id_type=MESH,
        )

    def to_near(src, dst, from_part, to_part, ss, rs, j, size=blk):
        return pltpu.make_async_remote_copy(
            src_ref=src.at[cut(from_part, size)], dst_ref=dst.at[cut(to_part, size)],
            send_sem=ss.at[j], recv_sem=rs.at[j],
            device_id={"dp": near(j)}, device_id_type=MESH,
        )

    def own_ad(j):
        return to_near(ad_send, ad_got, near(j), me, ad_ss, ad_rs, j)

    def mirror_ad(j):
        return to_near(ad_send, ad_got, far(near(j)), opposite, far_ss, far_rs, j)

    def far_request(j):
        return to_near(request, req_far, far(near(j)), me, reqf_ss, reqf_rs, j, 8)

    piece = n_ad // 2 // PIECES

    def piece_rows(c):
        return pl.ds(pl.multiple_of((group * PIECES + c) * piece, piece), piece)

    def across(c, which):
        r = piece_rows(c)
        src = down.at[r] if which == 0 else up.at[r, pl.ds(column, half_out)]
        cols = pl.ds(0, half_d) if which == 0 else pl.ds(half_d, half_out)
        return pltpu.make_async_remote_copy(
            src_ref=src, dst_ref=mirror.at[r, cols],
            send_sem=mir_ss.at[which, c], recv_sem=mir_rs.at[which, c],
            device_id={"dp": opposite}, device_id_type=MESH,
        )

    def share(c):
        r = piece_rows(c)
        return pltpu.make_async_remote_copy(
            src_ref=mirror.at[r], dst_ref=mirror.at[r],
            send_sem=x_ss.at[c], recv_sem=x_rs.at[c],
            device_id={"groups": 1 - group}, device_id_type=MESH,
        )

    req_far[...] = jnp.zeros_like(req_far)
    barrier = pltpu.get_barrier_semaphore()

    @pl.loop(1, dp)
    def _(k):
        pl.semaphore_signal(barrier, 1, device_id={"dp": peer(k)}, device_id_type=MESH)

    pl.semaphore_signal(barrier, 1, device_id={"tensor": 1 - core}, device_id_type=MESH)
    pl.semaphore_signal(barrier, 1, device_id={"groups": 1 - group}, device_id_type=MESH)
    pl.semaphore_wait(barrier, dp + 1)

    @pl.loop(1, dp)
    def _(k):
        send(request, req_got, req_ss, req_rs, k, 8).start()

    @pl.loop(1, half)
    def _(j):
        far_request(j).start()

    @pl.loop(0, PIECES)
    def _(c):
        across(c, 0).start()
        across(c, 1).start()

    req_got[cut(me, 8)] = request[cut(me, 8)]
    req_far[cut(me, 8)] = request[cut(opposite, 8)]

    def pack(lhs, wide, narrow, narrow_cols, dst, drow):
        @pl.loop(0, tiles)
        def _(j):
            c = pl.ds(pl.multiple_of(j * tile, tile), tile)
            dst[cut(drow), c] = mm(lhs, wide[:, c]).astype(BF)

        dst[cut(drow), half_d:] = mm(lhs, narrow[:, narrow_cols]).astype(BF)

    def place_of(p):
        i = lax.broadcasted_iota(jnp.int32, (blk, rows), 0) + p * blk
        return jnp.where(i == dest[...], 1.0, 0.0).astype(BF)

    def pack_tok(k, dst):
        p = peer(k)
        pack(place_of(p), tokens, cot, pl.ds(column, half_out), dst, p)

    @pl.loop(1, dp)
    def _(k):
        send(request, req_got, req_ss, req_rs, k, 8).wait()

    @pl.loop(1, half)
    def _(j):
        far_request(j).wait()

    def wanted(p, n, req_got=req_got):
        i = lax.broadcasted_iota(jnp.int32, (n, dp * 8), 0)
        j = lax.broadcasted_iota(jnp.int32, (n, dp * 8), 1)
        if p is None:
            hit = j == (i // blk) * 8 + (i % blk) // rank
        else:
            hit = j == p * 8 + i // rank
        return mm(jnp.where(hit, 1.0, 0.0).astype(BF), req_got[...].astype(BF))

    def pack_ad(p, req, wide, narrow, narrow_cols, dst, drow):
        i = lax.broadcasted_iota(jnp.int32, (blk, n_ad), 0)
        j = lax.broadcasted_iota(jnp.int32, (blk, n_ad), 1)
        source = wanted(p, blk, req) * float(rank) + (i % rank).astype(F32)
        lhs = jnp.where(source == j.astype(F32), 1.0, 0.0).astype(BF)
        pack(lhs, wide, narrow, narrow_cols, dst, drow)

    def pack_own(p, dst, drow):
        pack_ad(p, req_got, down, up, pl.ds(column, half_out), dst, drow)

    def pack_mirror(p, dst, drow):
        pack_ad(p, req_far, mirror, mirror, pl.ds(half_d, half_out), dst, drow)

    @pl.loop(1, half)
    def _(j):
        pack_own(near(j), ad_send, near(j))
        own_ad(j).start()

    def far_tok(j):
        return send(tok_send, tok_got, tok_ss, tok_rs, step(far(near(j))))

    def near_toks(when):
        if when == NEAR:
            @pl.loop(1, half)
            def _(j):
                send(tok_send, tok_got, tok_ss, tok_rs, step(near(j))).start()

    @pl.loop(0, EARLY)
    def _(j):
        pack_tok(step(far(near(j))), tok_send)
        far_tok(j).start()

    @pl.loop(EARLY, half)
    def _(j):
        pack_tok(step(far(near(j))), tok_send)

    @pl.loop(1, half)
    def _(j):
        pack_tok(step(near(j)), tok_send)

    near_toks(0)

    pack_tok(0, tok_got)
    pack_own(me, ad_got, me)

    base[...] = jnp.zeros_like(base)

    @pl.loop(0, tiles)
    def _(j):
        c = pl.ds(pl.multiple_of(j * tile, tile), tile)
        base[0] += mm(tokens[:, c], weight[c, pl.ds(column, half_out)])
        base[1] += mm(tokens[:, c], weight[c, pl.ds(other, half_out)])

    swap_base = to_core(base.at[1], base_got, 0)
    swap_base.start()

    @pl.loop(0, tiles)
    def _(j):
        c = pl.ds(pl.multiple_of(j * tile, tile), tile)
        frozen[:, c] = mm(cot[...], weight[c, :], 1, 1)

    @pl.loop(0, PIECES)
    def _(c):
        across(c, 0).wait()
        across(c, 1).wait()
        share(c).start()

    @pl.loop(EARLY, MIDDLE)
    def _(j):
        far_tok(j).start()

    near_toks(1)

    @pl.loop(0, PIECES)
    def _(c):
        share(c).wait()

    @pl.loop(1, half)
    def _(j):
        pack_mirror(near(j), ad_send, far(near(j)))
        mirror_ad(j).start()

    pack_mirror(me, ad_got, opposite)

    @pl.loop(1, half)
    def _(j):
        own_ad(j).wait()

    s_full[...] = jnp.zeros_like(s_full)

    def scores(from_part):
        r = pl.ds(pl.multiple_of(from_part * blk, half * blk), half * blk)

        @pl.loop(0, tiles)
        def _(j):
            c = pl.ds(pl.multiple_of(j * tile, tile), tile)
            s_full[:, r] += mm(tokens[:, c], ad_got[r, c], 1, 1)

    scores(first)

    @pl.loop(1, half)
    def _(j):
        mirror_ad(j).wait_send()

    near_toks(2)

    @pl.loop(MIDDLE, half)
    def _(j):
        far_tok(j).start()

    @pl.loop(1, half)
    def _(j):
        mirror_ad(j).wait_recv()

    near_toks(3)
    scores(half - first)

    n_rank = ad_got.shape[0]
    own_block = placed_row[...] == lax.broadcasted_iota(jnp.int32, (rows, n_rank), 1) // rank
    def lane_map(shape, lane_axis, shift):
        lane = lax.broadcasted_iota(jnp.int32, shape, lane_axis)
        i = lax.broadcasted_iota(jnp.int32, shape, 1 - lane_axis)
        return jnp.where(lane == i % rank + shift, 1.0, 0.0)

    def compact(full, shift):
        return mm(
            jnp.where(own_block, full, 0.0), lane_map((n_rank, 128), 1, shift),
            precision=lax.Precision.HIGHEST,
        )

    t_full = mm(cot[:, pl.ds(column, half_out)], ad_got[:, half_d:], 1, 1)
    part[...] = compact(s_full[...], 0) + compact(t_full, rank)
    swap_part = to_core(part, part_got, 1)
    swap_part.start()
    swap_part.wait()
    lanes = lax.broadcasted_iota(jnp.int32, part.shape, 1)
    factor = jnp.where(lanes < rank, 1.0, adapter_scale) * live[...]
    both[...] = ((part[...] + part_got[...]) * factor).astype(BF)

    @pl.loop(1, dp)
    def _(k):
        p = peer(k)
        both_send[cut(p)] = mm(place_of(p), both[...]).astype(BF)
        send(both_send, both_got, both_ss, both_rs, k).start()

    both_got[cut(me)] = mm(place_of(me), both[...]).astype(BF)

    def widen(shift):
        wide = mm(both[...], lane_map((128, n_rank), 0, shift).astype(BF))
        return jnp.where(own_block, wide, 0.0).astype(BF)

    shrunk_wide = widen(0)
    d_wide = widen(rank)
    swap_base.wait()
    extra = mm(shrunk_wide, ad_got[:, half_d:])
    output[...] = (base[0] + base_got[...] + adapter_scale * extra).astype(BF)

    @pl.loop(0, tiles)
    def _(j):
        c = pl.ds(pl.multiple_of(j * tile, tile), tile)
        input_gradient[:, c] = (frozen[:, c] + mm(d_wide, ad_got[:, c])).astype(BF)

    @pl.loop(1, dp)
    def _(k):
        send(both_send, both_got, both_ss, both_rs, k).wait()

    n_tok = tok_got.shape[0]
    ad_i = lax.broadcasted_iota(jnp.int32, (n_tok, n_ad), 1) // rank
    ad_block = wanted(None, n_tok) == ad_i.astype(F32)

    def widen_ad(shift):
        wide = mm(both_got[...], lane_map((128, n_ad), 0, shift).astype(BF))
        return jnp.where(ad_block, wide, 0.0).T.astype(BF)

    s_ad = widen_ad(0)
    d_ad = widen_ad(rank)

    @pl.loop(1, dp)
    def _(k):
        send(tok_send, tok_got, tok_ss, tok_rs, k).wait()

    @pl.loop(0, tiles)
    def _(j):
        c = pl.ds(pl.multiple_of(j * tile, tile), tile)
        grad_down[:, c] = mm(d_ad, tok_got[:, c]).astype(BF)

    grad_up[...] = (adapter_scale * mm(s_ad, tok_got[:, half_d:])).astype(BF)


PIECES = 4
EARLY = 1
MIDDLE = 2
NEAR = 2


def local(tokens, weight, down, up, index, length, cot):
    dp = lax.axis_size("dp")
    seg_dev = index.shape[0]
    rows, half_d = tokens.shape
    seg_len = rows // seg_dev
    n_own, rank, full_out = up.shape
    half_out = full_out // lax.axis_size("tensor")
    per_owner = max(1, -(-seg_dev // dp))
    n_ad = n_own * rank
    if dp * per_owner != seg_dev or per_owner > 8 or rank != seg_len or n_ad % 128 or n_own > 256 or n_ad % (32 * PIECES) or dp % 2 or (dp // 2 * per_owner * seg_len) % 128 or lax.axis_size("groups") != 2:
        return local_ops(tokens, weight, down, up, index, length, cot)
    owners = index // n_own
    local_index = index - owners * n_own
    pos = jnp.arange(seg_dev, dtype=jnp.int32)
    earlier = (owners[:, None] == owners[None, :]) & (pos[None, :] < pos[:, None])
    placed = owners * per_owner + jnp.sum(earlier.astype(jnp.int32), axis=1)
    slot8 = placed // per_owner * 8 + placed % per_owner
    hit = slot8[None, :] == jnp.arange(dp * 8, dtype=jnp.int32)[:, None]
    request = jnp.sum(jnp.where(hit, local_index[None, :] + 1, 0), axis=1) - 1
    request = jnp.broadcast_to(request.astype(F32)[:, None], (dp * 8, n_ad))
    row_i = jnp.arange(rows, dtype=jnp.int32)
    placed_row = jnp.repeat(placed, seg_len)
    dest = (placed_row * seg_len + row_i % seg_len)[None, :]
    live = (row_i % seg_len < jnp.repeat(length, seg_len)).astype(F32)[:, None]
    wide = half_d + half_out
    tile = 512 if half_d % 512 == 0 else 128
    vmem = pl.BlockSpec(memory_space=pltpu.VMEM)
    dma = pltpu.SemaphoreType.DMA((dp,))
    outs = pl.pallas_call(
        functools.partial(kernel, dp, per_owner, seg_len, rank, tile),
        out_shape=[
            jax.ShapeDtypeStruct((rows, half_out), BF),
            jax.ShapeDtypeStruct((rows, half_d), BF),
            jax.ShapeDtypeStruct((n_ad, half_d), BF),
            jax.ShapeDtypeStruct((n_ad, half_out), BF),
        ],
        in_specs=[vmem] * 9,
        out_specs=[vmem] * 4,
        scratch_shapes=[
            pltpu.VMEM((rows, wide), BF),
            pltpu.VMEM((rows, wide), BF),
            pltpu.VMEM((rows, wide), BF),
            pltpu.VMEM((rows, wide), BF),
            pltpu.VMEM((dp * 8, n_ad), F32),
            pltpu.VMEM((rows, 128), BF),
            pltpu.VMEM((rows, 128), BF),
            pltpu.VMEM((rows, 128), BF),
            pltpu.VMEM((2, rows, half_out), F32),
            pltpu.VMEM((rows, half_out), F32),
            pltpu.VMEM((rows, 128), F32),
            pltpu.VMEM((rows, 128), F32),
            pltpu.VMEM((rows, rows), F32),
            pltpu.VMEM((n_ad, wide), BF),
            pltpu.VMEM((dp * 8, n_ad), F32),
            pltpu.VMEM((rows, half_d), F32),
            dma, dma, dma, dma, dma, dma, dma, dma,
            pltpu.SemaphoreType.DMA((2,)),
            pltpu.SemaphoreType.DMA((2,)),
            pltpu.SemaphoreType.DMA((2, PIECES)),
            pltpu.SemaphoreType.DMA((2, PIECES)),
            dma, dma,
            pltpu.SemaphoreType.DMA((PIECES,)),
            pltpu.SemaphoreType.DMA((PIECES,)),
            dma, dma,
        ],
        compiler_params=pltpu.CompilerParams(
            collective_id=0, has_side_effects=True, vmem_limit_bytes=56 * 2**20
        ),
        cost_estimate=pl.CostEstimate(
            flops=8 * rows * half_d * full_out, bytes_accessed=16 * rows * half_d, transcendentals=0
        ),
    )(
        tokens, weight, down.reshape(n_ad, half_d), up.reshape(n_ad, full_out),
        cot, dest, placed_row[:, None], live, request,
    )
    output, input_gradient, grad_down, grad_up = outs
    return (
        output, input_gradient,
        grad_down.reshape(n_own, rank, half_d), grad_up.reshape(n_own, rank, half_out),
    )


def solution(mesh):
    in_specs = (
        P(("groups", "dp"), "tensor"),
        P("tensor", None),
        P("dp", None, "tensor"),
        P("dp", None, None),
        P(("groups", "dp")),
        P(("groups", "dp")),
        P(("groups", "dp"), None),
    )
    out_specs = (
        P(("groups", "dp"), "tensor"),
        P(("groups", "dp"), "tensor"),
        P(("groups", "dp"), None, "tensor"),
        P(("groups", "dp"), None, "tensor"),
    )
    return jax.shard_map(local, mesh=mesh, in_specs=in_specs, out_specs=out_specs, check_vma=False)
```

```python
import functools

import jax
import jax.numpy as jnp
from jax import lax
from jax.experimental import pallas as pl
from jax.experimental.pallas import tpu as pltpu
from jax.sharding import PartitionSpec as P

adapter_scale = 2.0
BF = jnp.bfloat16
F32 = jnp.float32


def mm(a, b, ca=1, cb=0, **kw):
    return lax.dot_general(
        a, b, (((ca,), (cb,)), ((), ())), preferred_element_type=F32, **kw
    )


def local_ops(tokens, weight, down, up, index, length, cot):
    dp = lax.axis_size("dp")
    seg_dev = index.shape[0]
    rows, half_d = tokens.shape
    seg_len = rows // seg_dev
    full_out = weight.shape[1]
    half_out = full_out // lax.axis_size("tensor")
    n_own, rank = down.shape[0], down.shape[1]
    per_owner = max(1, -(-seg_dev // dp))
    n_slots = dp * per_owner
    n_tok, n_rank, n_ad = n_slots * seg_len, n_slots * rank, n_own * rank
    column = lax.axis_index("tensor") * half_out

    owners = index // n_own
    local_index = index - owners * n_own
    pos = jnp.arange(seg_dev, dtype=jnp.int32)
    earlier = (owners[:, None] == owners[None, :]) & (pos[None, :] < pos[:, None])
    placed = owners * per_owner + jnp.sum(earlier.astype(jnp.int32), axis=1)
    picker = placed[None, :] == jnp.arange(n_slots, dtype=jnp.int32)[:, None]
    request = jnp.sum(jnp.where(picker, local_index[None, :] + 1, 0), axis=1)
    requested = (
        lax.all_to_all(
            request.reshape(dp, per_owner), "dp", split_axis=0, concat_axis=0, tiled=True
        ).reshape(n_slots)
        - 1
    )

    row_i = jnp.arange(rows, dtype=jnp.int32)
    placed_row = jnp.repeat(placed, seg_len)
    dest = placed_row * seg_len + row_i % seg_len
    live = (row_i % seg_len < jnp.repeat(length, seg_len)).astype(F32)[:, None]
    tok_i = jnp.arange(n_tok, dtype=jnp.int32)
    rank_i = jnp.arange(n_rank, dtype=jnp.int32)
    ad_i = jnp.arange(n_ad, dtype=jnp.int32)
    r_i = jnp.arange(rank, dtype=jnp.int32)
    place = (tok_i[:, None] == dest[None, :]).astype(BF)
    source = jnp.repeat(requested, rank) * rank + rank_i % rank
    choose = (source[:, None] == ad_i[None, :]).astype(BF)
    own_block = placed_row[:, None] == (rank_i // rank)[None, :]
    ad_block = jnp.repeat(requested, seg_len)[:, None] == (ad_i // rank)[None, :]
    spread = (rank_i[None, :] % rank == r_i[:, None]).astype(BF)
    spread_ad = (ad_i[None, :] % rank == r_i[:, None]).astype(BF)

    def exchange(x):
        y = lax.all_to_all(
            x.reshape(dp, x.shape[0] // dp, x.shape[1]),
            "dp", split_axis=0, concat_axis=0, tiled=True,
        )
        return y.reshape(x.shape)

    cot_half = lax.dynamic_slice_in_dim(cot, column, half_out, 1)
    up2 = lax.dynamic_slice_in_dim(up.reshape(n_ad, full_out), column, half_out, 1)
    tok_got = exchange(mm(place, tokens).astype(BF))
    cot_got = exchange(mm(place, cot_half).astype(BF))
    up_got = exchange(mm(choose, up2).astype(BF))
    down_got = exchange(mm(choose, down.reshape(n_ad, half_d)).astype(BF))

    base = lax.psum_scatter(mm(tokens, weight), "tensor", scatter_dimension=1, tiled=True)

    def compact(full):
        masked = jnp.where(own_block, full, 0.0)
        return mm(masked, spread.astype(F32), 1, 1, precision=lax.Precision.HIGHEST)

    parts = jnp.concatenate(
        [compact(mm(tokens, down_got, 1, 1)), compact(mm(cot_half, up_got, 1, 1))], axis=1
    )
    sums = lax.psum(parts, "tensor") * live
    shrunk = sums[:, :rank].astype(BF)
    d_shrunk = (adapter_scale * sums[:, rank:]).astype(BF)
    both = jnp.concatenate([shrunk, d_shrunk], axis=1)
    both_got = exchange(mm(place, both).astype(BF))

    shrunk_wide = jnp.where(own_block, mm(shrunk, spread), 0.0).astype(BF)
    d_wide = jnp.where(own_block, mm(d_shrunk, spread), 0.0).astype(BF)
    output = (base + adapter_scale * mm(shrunk_wide, up_got)).astype(BF)
    input_gradient = (mm(cot, weight, 1, 1) + mm(d_wide, down_got)).astype(BF)

    s_ad = jnp.where(ad_block, mm(both_got[:, :rank], spread_ad), 0.0).astype(BF)
    d_ad = jnp.where(ad_block, mm(both_got[:, rank:], spread_ad), 0.0).astype(BF)
    grad_down = mm(d_ad, tok_got, 0, 0).astype(BF).reshape(n_own, rank, half_d)
    grad_up = (adapter_scale * mm(s_ad, cot_got, 0, 0)).astype(BF)
    return output, input_gradient, grad_down, grad_up.reshape(n_own, rank, half_out)

MESH = pl.DeviceIdType.MESH


def kernel(
    dp, per_owner, seg_len, rank, tile,
    tokens, weight, down, up, cot, dest, placed_row, live, request,
    output, input_gradient, grad_down, grad_up,
    tok_send, tok_got, ad_send, ad_got, req_got, both, both_send, both_got,
    base, base_got, part, part_got, s_full, mirror, req_far, frozen,
    req_ss, req_rs, ad_ss, ad_rs, tok_ss, tok_rs, both_ss, both_rs, core_ss, core_rs,
    mir_ss, mir_rs, far_ss, far_rs, x_ss, x_rs, reqf_ss, reqf_rs,
):
    me = lax.axis_index("dp")
    core = lax.axis_index("tensor")
    group = lax.axis_index("groups")
    half = dp // 2
    first = me // half * half
    opposite = lax.rem(me + half, dp)
    rows, half_d = tokens.shape
    n_ad = down.shape[0]
    half_out = output.shape[1]
    blk = per_owner * seg_len
    tiles = half_d // tile
    column = pl.multiple_of(core * half_out, 128)
    other = pl.multiple_of((1 - core) * half_out, 128)

    def peer(k):
        return lax.rem(me + k, dp)

    def near(j):
        return first + lax.rem(me - first + j, half)

    def far(p):
        return lax.rem(p + half, dp)

    def step(p):
        return lax.rem(p - me + dp, dp)

    def cut(p, size=blk):
        return pl.ds(pl.multiple_of(p * size, size), size)

    def send(src, dst, ss, rs, k, size=blk):
        p = peer(k)
        return pltpu.make_async_remote_copy(
            src_ref=src.at[cut(p, size)], dst_ref=dst.at[cut(me, size)],
            send_sem=ss.at[k], recv_sem=rs.at[k],
            device_id={"dp": p}, device_id_type=MESH,
        )

    def to_core(src, dst, i):
        return pltpu.make_async_remote_copy(
            src_ref=src, dst_ref=dst, send_sem=core_ss.at[i], recv_sem=core_rs.at[i],
            device_id={"tensor": 1 - core}, device_id_type=MESH,
        )

    def to_near(src, dst, from_part, to_part, ss, rs, j, size=blk):
        return pltpu.make_async_remote_copy(
            src_ref=src.at[cut(from_part, size)], dst_ref=dst.at[cut(to_part, size)],
            send_sem=ss.at[j], recv_sem=rs.at[j],
            device_id={"dp": near(j)}, device_id_type=MESH,
        )

    def own_ad(j):
        return to_near(ad_send, ad_got, near(j), me, ad_ss, ad_rs, j)

    def mirror_ad(j):
        return to_near(ad_send, ad_got, far(near(j)), opposite, far_ss, far_rs, j)

    def far_request(j):
        return to_near(request, req_far, far(near(j)), me, reqf_ss, reqf_rs, j, 8)

    piece = n_ad // 2 // PIECES

    def piece_rows(c):
        return pl.ds(pl.multiple_of((group * PIECES + c) * piece, piece), piece)

    def across(c, which):
        r = piece_rows(c)
        src = down.at[r] if which == 0 else up.at[r, pl.ds(column, half_out)]
        cols = pl.ds(0, half_d) if which == 0 else pl.ds(half_d, half_out)
        return pltpu.make_async_remote_copy(
            src_ref=src, dst_ref=mirror.at[r, cols],
            send_sem=mir_ss.at[which, c], recv_sem=mir_rs.at[which, c],
            device_id={"dp": opposite}, device_id_type=MESH,
        )

    def share(c):
        r = piece_rows(c)
        return pltpu.make_async_remote_copy(
            src_ref=mirror.at[r], dst_ref=mirror.at[r],
            send_sem=x_ss.at[c], recv_sem=x_rs.at[c],
            device_id={"groups": 1 - group}, device_id_type=MESH,
        )

    req_far[...] = jnp.zeros_like(req_far)
    barrier = pltpu.get_barrier_semaphore()

    @pl.loop(1, dp)
    def _(k):
        pl.semaphore_signal(barrier, 1, device_id={"dp": peer(k)}, device_id_type=MESH)

    pl.semaphore_signal(barrier, 1, device_id={"tensor": 1 - core}, device_id_type=MESH)
    pl.semaphore_signal(barrier, 1, device_id={"groups": 1 - group}, device_id_type=MESH)
    pl.semaphore_wait(barrier, dp + 1)

    @pl.loop(1, dp)
    def _(k):
        send(request, req_got, req_ss, req_rs, k, 8).start()

    @pl.loop(1, half)
    def _(j):
        far_request(j).start()

    @pl.loop(0, PIECES)
    def _(c):
        across(c, 0).start()
        across(c, 1).start()

    req_got[cut(me, 8)] = request[cut(me, 8)]
    req_far[cut(me, 8)] = request[cut(opposite, 8)]

    def pack(lhs, wide, narrow, narrow_cols, dst, drow):
        @pl.loop(0, tiles)
        def _(j):
            c = pl.ds(pl.multiple_of(j * tile, tile), tile)
            dst[cut(drow), c] = mm(lhs, wide[:, c]).astype(BF)

        dst[cut(drow), half_d:] = mm(lhs, narrow[:, narrow_cols]).astype(BF)

    def place_of(p):
        i = lax.broadcasted_iota(jnp.int32, (blk, rows), 0) + p * blk
        return jnp.where(i == dest[...], 1.0, 0.0).astype(BF)

    def pack_tok(k, dst):
        p = peer(k)
        pack(place_of(p), tokens, cot, pl.ds(column, half_out), dst, p)

    @pl.loop(1, dp)
    def _(k):
        send(request, req_got, req_ss, req_rs, k, 8).wait()

    @pl.loop(1, half)
    def _(j):
        far_request(j).wait()

    def wanted(p, n, req_got=req_got):
        i = lax.broadcasted_iota(jnp.int32, (n, dp * 8), 0)
        j = lax.broadcasted_iota(jnp.int32, (n, dp * 8), 1)
        if p is None:
            hit = j == (i // blk) * 8 + (i % blk) // rank
        else:
            hit = j == p * 8 + i // rank
        return mm(jnp.where(hit, 1.0, 0.0).astype(BF), req_got[...].astype(BF))

    def pack_ad(p, req, wide, narrow, narrow_cols, dst, drow):
        i = lax.broadcasted_iota(jnp.int32, (blk, n_ad), 0)
        j = lax.broadcasted_iota(jnp.int32, (blk, n_ad), 1)
        source = wanted(p, blk, req) * float(rank) + (i % rank).astype(F32)
        lhs = jnp.where(source == j.astype(F32), 1.0, 0.0).astype(BF)
        pack(lhs, wide, narrow, narrow_cols, dst, drow)

    def pack_own(p, dst, drow):
        pack_ad(p, req_got, down, up, pl.ds(column, half_out), dst, drow)

    def pack_mirror(p, dst, drow):
        pack_ad(p, req_far, mirror, mirror, pl.ds(half_d, half_out), dst, drow)

    @pl.loop(1, half)
    def _(j):
        pack_own(near(j), ad_send, near(j))
        own_ad(j).start()

    def far_tok(j):
        return send(tok_send, tok_got, tok_ss, tok_rs, step(far(near(j))))

    def near_toks(when):
        if when == NEAR:
            @pl.loop(1, half)
            def _(j):
                send(tok_send, tok_got, tok_ss, tok_rs, step(near(j))).start()

    @pl.loop(0, EARLY)
    def _(j):
        pack_tok(step(far(near(j))), tok_send)
        far_tok(j).start()

    @pl.loop(EARLY, half)
    def _(j):
        pack_tok(step(far(near(j))), tok_send)

    @pl.loop(1, half)
    def _(j):
        pack_tok(step(near(j)), tok_send)

    near_toks(0)

    pack_tok(0, tok_got)
    pack_own(me, ad_got, me)

    base[...] = jnp.zeros_like(base)

    @pl.loop(0, tiles)
    def _(j):
        c = pl.ds(pl.multiple_of(j * tile, tile), tile)
        base[0] += mm(tokens[:, c], weight[c, pl.ds(column, half_out)])
        base[1] += mm(tokens[:, c], weight[c, pl.ds(other, half_out)])

    swap_base = to_core(base.at[1], base_got, 0)
    swap_base.start()

    @pl.loop(0, tiles)
    def _(j):
        c = pl.ds(pl.multiple_of(j * tile, tile), tile)
        frozen[:, c] = mm(cot[...], weight[c, :], 1, 1)

    @pl.loop(0, PIECES)
    def _(c):
        across(c, 0).wait()
        across(c, 1).wait()
        share(c).start()

    @pl.loop(EARLY, MIDDLE)
    def _(j):
        far_tok(j).start()

    near_toks(1)

    @pl.loop(0, PIECES)
    def _(c):
        share(c).wait()

    @pl.loop(1, half)
    def _(j):
        pack_mirror(near(j), ad_send, far(near(j)))
        mirror_ad(j).start()

    pack_mirror(me, ad_got, opposite)

    @pl.loop(1, half)
    def _(j):
        own_ad(j).wait()

    s_full[...] = jnp.zeros_like(s_full)

    def scores(from_part):
        r = pl.ds(pl.multiple_of(from_part * blk, half * blk), half * blk)

        @pl.loop(0, tiles)
        def _(j):
            c = pl.ds(pl.multiple_of(j * tile, tile), tile)
            s_full[:, r] += mm(tokens[:, c], ad_got[r, c], 1, 1)

    scores(first)

    @pl.loop(1, half)
    def _(j):
        mirror_ad(j).wait_send()

    near_toks(2)

    @pl.loop(MIDDLE, half)
    def _(j):
        far_tok(j).start()

    @pl.loop(1, half)
    def _(j):
        mirror_ad(j).wait_recv()

    near_toks(3)
    scores(half - first)

    n_rank = ad_got.shape[0]
    own_block = placed_row[...] == lax.broadcasted_iota(jnp.int32, (rows, n_rank), 1) // rank
    def lane_map(shape, lane_axis, shift):
        lane = lax.broadcasted_iota(jnp.int32, shape, lane_axis)
        i = lax.broadcasted_iota(jnp.int32, shape, 1 - lane_axis)
        return jnp.where(lane == i % rank + shift, 1.0, 0.0)

    def compact(full, shift):
        return mm(
            jnp.where(own_block, full, 0.0), lane_map((n_rank, 128), 1, shift),
            precision=lax.Precision.HIGHEST,
        )

    t_full = mm(cot[:, pl.ds(column, half_out)], ad_got[:, half_d:], 1, 1)
    part[...] = compact(s_full[...], 0) + compact(t_full, rank)
    swap_part = to_core(part, part_got, 1)
    swap_part.start()
    swap_part.wait()
    lanes = lax.broadcasted_iota(jnp.int32, part.shape, 1)
    factor = jnp.where(lanes < rank, 1.0, adapter_scale) * live[...]
    both[...] = ((part[...] + part_got[...]) * factor).astype(BF)

    @pl.loop(1, dp)
    def _(k):
        p = peer(k)
        both_send[cut(p)] = mm(place_of(p), both[...]).astype(BF)
        send(both_send, both_got, both_ss, both_rs, k).start()

    both_got[cut(me)] = mm(place_of(me), both[...]).astype(BF)

    def widen(shift):
        wide = mm(both[...], lane_map((128, n_rank), 0, shift).astype(BF))
        return jnp.where(own_block, wide, 0.0).astype(BF)

    shrunk_wide = widen(0)
    d_wide = widen(rank)
    swap_base.wait()
    extra = mm(shrunk_wide, ad_got[:, half_d:])
    output[...] = (base[0] + base_got[...] + adapter_scale * extra).astype(BF)

    @pl.loop(0, tiles)
    def _(j):
        c = pl.ds(pl.multiple_of(j * tile, tile), tile)
        input_gradient[:, c] = (frozen[:, c] + mm(d_wide, ad_got[:, c])).astype(BF)

    @pl.loop(1, dp)
    def _(k):
        send(both_send, both_got, both_ss, both_rs, k).wait()

    n_tok = tok_got.shape[0]
    ad_i = lax.broadcasted_iota(jnp.int32, (n_tok, n_ad), 1) // rank
    ad_block = wanted(None, n_tok) == ad_i.astype(F32)

    def widen_ad(shift):
        wide = mm(both_got[...], lane_map((128, n_ad), 0, shift).astype(BF))
        return jnp.where(ad_block, wide, 0.0).T.astype(BF)

    s_ad = widen_ad(0)
    d_ad = widen_ad(rank)

    @pl.loop(1, dp)
    def _(k):
        send(tok_send, tok_got, tok_ss, tok_rs, k).wait()

    @pl.loop(0, tiles)
    def _(j):
        c = pl.ds(pl.multiple_of(j * tile, tile), tile)
        grad_down[:, c] = mm(d_ad, tok_got[:, c]).astype(BF)

    grad_up[...] = (adapter_scale * mm(s_ad, tok_got[:, half_d:])).astype(BF)


PIECES = 8
EARLY = 1
MIDDLE = 2
NEAR = 2


def local(tokens, weight, down, up, index, length, cot):
    dp = lax.axis_size("dp")
    seg_dev = index.shape[0]
    rows, half_d = tokens.shape
    seg_len = rows // seg_dev
    n_own, rank, full_out = up.shape
    half_out = full_out // lax.axis_size("tensor")
    per_owner = max(1, -(-seg_dev // dp))
    n_ad = n_own * rank
    if dp * per_owner != seg_dev or per_owner > 8 or rank != seg_len or n_ad % 128 or n_own > 256 or n_ad % (32 * PIECES) or dp % 2 or (dp // 2 * per_owner * seg_len) % 128 or lax.axis_size("groups") != 2:
        return local_ops(tokens, weight, down, up, index, length, cot)
    owners = index // n_own
    local_index = index - owners * n_own
    pos = jnp.arange(seg_dev, dtype=jnp.int32)
    earlier = (owners[:, None] == owners[None, :]) & (pos[None, :] < pos[:, None])
    placed = owners * per_owner + jnp.sum(earlier.astype(jnp.int32), axis=1)
    slot8 = placed // per_owner * 8 + placed % per_owner
    hit = slot8[None, :] == jnp.arange(dp * 8, dtype=jnp.int32)[:, None]
    request = jnp.sum(jnp.where(hit, local_index[None, :] + 1, 0), axis=1) - 1
    request = jnp.broadcast_to(request.astype(F32)[:, None], (dp * 8, n_ad))
    row_i = jnp.arange(rows, dtype=jnp.int32)
    placed_row = jnp.repeat(placed, seg_len)
    dest = (placed_row * seg_len + row_i % seg_len)[None, :]
    live = (row_i % seg_len < jnp.repeat(length, seg_len)).astype(F32)[:, None]
    wide = half_d + half_out
    tile = 512 if half_d % 512 == 0 else 128
    vmem = pl.BlockSpec(memory_space=pltpu.VMEM)
    dma = pltpu.SemaphoreType.DMA((dp,))
    outs = pl.pallas_call(
        functools.partial(kernel, dp, per_owner, seg_len, rank, tile),
        out_shape=[
            jax.ShapeDtypeStruct((rows, half_out), BF),
            jax.ShapeDtypeStruct((rows, half_d), BF),
            jax.ShapeDtypeStruct((n_ad, half_d), BF),
            jax.ShapeDtypeStruct((n_ad, half_out), BF),
        ],
        in_specs=[vmem] * 9,
        out_specs=[vmem] * 4,
        scratch_shapes=[
            pltpu.VMEM((rows, wide), BF),
            pltpu.VMEM((rows, wide), BF),
            pltpu.VMEM((rows, wide), BF),
            pltpu.VMEM((rows, wide), BF),
            pltpu.VMEM((dp * 8, n_ad), F32),
            pltpu.VMEM((rows, 128), BF),
            pltpu.VMEM((rows, 128), BF),
            pltpu.VMEM((rows, 128), BF),
            pltpu.VMEM((2, rows, half_out), F32),
            pltpu.VMEM((rows, half_out), F32),
            pltpu.VMEM((rows, 128), F32),
            pltpu.VMEM((rows, 128), F32),
            pltpu.VMEM((rows, rows), F32),
            pltpu.VMEM((n_ad, wide), BF),
            pltpu.VMEM((dp * 8, n_ad), F32),
            pltpu.VMEM((rows, half_d), F32),
            dma, dma, dma, dma, dma, dma, dma, dma,
            pltpu.SemaphoreType.DMA((2,)),
            pltpu.SemaphoreType.DMA((2,)),
            pltpu.SemaphoreType.DMA((2, PIECES)),
            pltpu.SemaphoreType.DMA((2, PIECES)),
            dma, dma,
            pltpu.SemaphoreType.DMA((PIECES,)),
            pltpu.SemaphoreType.DMA((PIECES,)),
            dma, dma,
        ],
        compiler_params=pltpu.CompilerParams(
            collective_id=0, has_side_effects=True, vmem_limit_bytes=56 * 2**20
        ),
        cost_estimate=pl.CostEstimate(
            flops=8 * rows * half_d * full_out, bytes_accessed=16 * rows * half_d, transcendentals=0
        ),
    )(
        tokens, weight, down.reshape(n_ad, half_d), up.reshape(n_ad, full_out),
        cot, dest, placed_row[:, None], live, request,
    )
    output, input_gradient, grad_down, grad_up = outs
    return (
        output, input_gradient,
        grad_down.reshape(n_own, rank, half_d), grad_up.reshape(n_own, rank, half_out),
    )


def solution(mesh):
    in_specs = (
        P(("groups", "dp"), "tensor"),
        P("tensor", None),
        P("dp", None, "tensor"),
        P("dp", None, None),
        P(("groups", "dp")),
        P(("groups", "dp")),
        P(("groups", "dp"), None),
    )
    out_specs = (
        P(("groups", "dp"), "tensor"),
        P(("groups", "dp"), "tensor"),
        P(("groups", "dp"), None, "tensor"),
        P(("groups", "dp"), None, "tensor"),
    )
    return jax.shard_map(local, mesh=mesh, in_specs=in_specs, out_specs=out_specs, check_vma=False)
```
